256 devices in a mesh: dp: 64 (over y, z, core), width: 4 (over x).
Axes of the slice: x: 4, y: 4, z: 8, core: 2. Of those that a mesh axis runs over, the one named last changes fastest.
Arguments:
- queries: bfloat16 [8192, 3584], P('dp', 'width'), may hold values from -8 to 8
- codes: bfloat16 [8192, 3584], P('dp', 'width'), may hold values from -8 to 8
- pairing: int32 [64, 128], P('dp'), may hold values from 0 to 127, each once within a row
- neg_blocks: int32 [64, 4], replicated, may hold values from 0 to 63, as said below
- neg_count: int32 [64], replicated, may hold values from 1 to 4
Outputs:
- grad_queries: float32 [8192, 3584], P('dp', 'width')
- grad_codes: float32 [8192, 3584], P('dp', 'width')
The draws below stay inside these ranges and needn't reach their ends.
Inputs may be any that keep to these rules, and one draw needn't show every extreme that they name: Row b of pairing orders 0 to 127, each once. `neg_blocks`: row b names 4 different blocks, none of them b.
All inputs are finite; a program needn't handle non-finite values.
Results may differ from the reference program's by a relative error of at most 0.0023.
Values may be sent and summed in bfloat16 or wider, within the bound.
No kernel may reach another device: no remote copies, remote signals or barrier semaphores. Data moves between devices by JAX's collectives and lax.ppermute only.
A program may use at most 64 MiB of HBM per device.

```python
import jax
import jax.numpy as jnp
from jax import lax

D = 3584
BLK = 128
NEG = 4
TOTAL_BLOCKS = 64
ROWS = 8192


def embed_pair(key):
    total = BLK * TOTAL_BLOCKS
    base = jax.random.fold_in(key, 7)
    key_q, key_c = jax.random.split(base, 2)
    norm_factor = 1.0 / D ** 0.5
    query_vals = jax.random.truncated_normal(key_q, -6.0, 6.0, (total, D), jnp.float32) * norm_factor
    code_vals = jax.random.truncated_normal(key_c, -6.0, 6.0, (total, D), jnp.float32) * norm_factor
    return (query_vals, code_vals)


def draw_queries(key, part):
    return embed_pair(key)[0].astype(jnp.bfloat16)


def draw_codes(key, part):
    return embed_pair(key)[1].astype(jnp.bfloat16)


def draw_neg_blocks(key, part):
    key_r, key_h = jax.random.split(jax.random.fold_in(key, 11))
    random_jitter = jax.random.randint(key_r, (TOTAL_BLOCKS, TOTAL_BLOCKS), 0, 4096)
    sorted_order = jax.random.permutation(key_h, TOTAL_BLOCKS)
    extra_reward = jnp.where(sorted_order < 4, 640, 0).astype(jnp.int32)
    column_pick = jnp.arange(TOTAL_BLOCKS, dtype=jnp.int32)
    block_ranking = (random_jitter + extra_reward[None, :]) * TOTAL_BLOCKS + column_pick[None, :]
    block_ranking = jnp.where(column_pick[:, None] == column_pick[None, :], -1, block_ranking)
    unused, chosen = lax.top_k(block_ranking, NEG)
    return chosen.astype(jnp.int32)


def draw_neg_count(key, part):
    key_c, key_b = jax.random.split(jax.random.fold_in(key, 13))
    counts = jax.random.randint(key_c, (TOTAL_BLOCKS,), 1, NEG + 1)
    first = jax.random.randint(key_b, (), 0, TOTAL_BLOCKS)
    counts = counts.at[first].set(NEG)
    counts = counts.at[(first + 1) % TOTAL_BLOCKS].set(1)
    return counts.astype(jnp.int32)


def setup_inputs(seed: int = 0) -> dict:
    key_list = jax.random.split(jax.random.key(seed), 6)
    return {
        "queries": draw_queries(jax.random.fold_in(key_list[5], 71), 0),
        "codes": draw_codes(jax.random.fold_in(key_list[5], 71), 0),
        "pairing": jax.vmap(lambda own: jax.random.permutation(own, BLK))(jax.random.split(key_list[2], TOTAL_BLOCKS)).reshape((TOTAL_BLOCKS, BLK)).astype(jnp.int32),
        "neg_blocks": draw_neg_blocks(jax.random.fold_in(key_list[5], 71), 0),
        "neg_count": draw_neg_count(jax.random.fold_in(key_list[5], 71), 0),
    }


INV_TEMP = 50.0


def coefficients(scores, targets, valid):
    masked_scores = jnp.where(valid, scores, -jnp.inf)
    top = jnp.max(masked_scores, axis=1, keepdims=True)
    expo = jnp.where(valid, jnp.exp(masked_scores - top), 0.0)
    probs = expo / jnp.sum(expo, axis=1, keepdims=True)
    return (0.5 * (probs - targets)).astype(jnp.bfloat16)


def reference(queries, codes, pairing, neg_blocks, neg_count):
    q_blocks = queries.reshape(TOTAL_BLOCKS, BLK, D)
    c_blocks = codes.reshape(TOTAL_BLOCKS, BLK, D)
    columns = jnp.arange((NEG + 1) * BLK, dtype=jnp.int32)
    slot_of = columns // BLK
    local_rows = jnp.arange(BLK, dtype=jnp.int32)

    def one_block(carry, index):
        grad_q, grad_c = carry
        own_q = q_blocks[index]
        own_c = c_blocks[index]
        ids = neg_blocks[index]
        count = neg_count[index]
        pos = pairing[index]
        far_q = q_blocks[ids].reshape(NEG * BLK, D)
        far_c = c_blocks[ids].reshape(NEG * BLK, D)
        all_q = jnp.concatenate([own_q, far_q], axis=0)
        all_c = jnp.concatenate([own_c, far_c], axis=0)
        score_one = INV_TEMP * jnp.dot(own_q, all_c.T, preferred_element_type=jnp.float32)
        score_two = jnp.concatenate([score_one[:, :BLK].T, INV_TEMP * jnp.dot(own_c, far_q.T, preferred_element_type=jnp.float32)], axis=1)
        valid = (slot_of <= count)[None, :]
        target_one = (columns[None, :] == pos[:, None]).astype(jnp.float32)
        pos_ext = jnp.concatenate([pos, jnp.full((NEG * BLK,), -1, jnp.int32)])
        target_two = (pos_ext[None, :] == local_rows[:, None]).astype(jnp.float32)
        coef_one = coefficients(score_one, target_one, valid)
        coef_two = coefficients(score_two, target_two, valid)
        grad_own_q = INV_TEMP * (jnp.dot(coef_one, all_c, preferred_element_type=jnp.float32) + jnp.dot(coef_two[:, :BLK].T, own_c, preferred_element_type=jnp.float32))
        grad_own_c = INV_TEMP * (jnp.dot(coef_two, all_q, preferred_element_type=jnp.float32) + jnp.dot(coef_one[:, :BLK].T, own_q, preferred_element_type=jnp.float32))
        tail_two = coef_two[:, BLK:].reshape(BLK, NEG, BLK).astype(jnp.float32)
        tail_one = coef_one[:, BLK:].reshape(BLK, NEG, BLK).astype(jnp.float32)
        far_grad_q = (INV_TEMP * jnp.einsum("jrn,jd->rnd", tail_two, own_c.astype(jnp.float32))).astype(jnp.bfloat16)
        far_grad_c = (INV_TEMP * jnp.einsum("jrn,jd->rnd", tail_one, own_q.astype(jnp.float32))).astype(jnp.bfloat16)
        live = (jnp.arange(NEG, dtype=jnp.int32) < count)[:, None, None]
        far_grad_q = jnp.where(live, far_grad_q.astype(jnp.float32), 0.0)
        far_grad_c = jnp.where(live, far_grad_c.astype(jnp.float32), 0.0)
        grad_q = grad_q.at[index].add(grad_own_q).at[ids].add(far_grad_q)
        grad_c = grad_c.at[index].add(grad_own_c).at[ids].add(far_grad_c)
        return (grad_q, grad_c), None

    start = (jnp.zeros((TOTAL_BLOCKS, BLK, D), jnp.float32), jnp.zeros((TOTAL_BLOCKS, BLK, D), jnp.float32))
    (grad_q, grad_c), unused = lax.scan(one_block, start, jnp.arange(TOTAL_BLOCKS, dtype=jnp.int32))
    return grad_q.reshape(ROWS, D), grad_c.reshape(ROWS, D)
```

```python
import functools

import jax
import jax.numpy as jnp
from jax import lax
from jax.experimental import pallas as pl
from jax.experimental.pallas import tpu as pltpu
from jax.sharding import Mesh, PartitionSpec as P

INV_TEMP = 50.0
NY, NZ, NC, NX = 4, 8, 2, 4
BLK = 128
SLOTS = 4
QUARTER = BLK // NX
HALF = BLK // 2
CAP_SMALL = 16
CAP_FULL = 80
LOWEST = -3.0e38
DP = ("y", "z", "c")
LIST_LEN = 88
F32 = jnp.float32
BF16 = jnp.bfloat16
VMEM = pltpu.VMEM
SMEM = pltpu.SMEM


def wrap(v, n):
    return v & (n - 1)


def spec_v():
    return pl.BlockSpec(memory_space=VMEM)


def spec_s():
    return pl.BlockSpec(memory_space=SMEM)


def list_kernel(neg_ref, count_ref, ent_ref):
    y, z, c, x = (lax.axis_index(name) for name in ("y", "z", "c", "x"))

    def push(k, e, j, take):
        ent_ref[0, k] = e
        ent_ref[1, k] = j
        return k + take.astype(jnp.int32)

    def first(e, k):
        b = ((y << 3) + wrap(z + e, NZ)) * NC + c
        count = count_ref[b]
        for r in range(SLOTS):
            n = neg_ref[b, r]
            take = (r < count) & (wrap(n >> 1, NZ) == z)
            k = push(k, e, 2 * wrap((n >> 4) - y, NY) + ((n & 1) ^ c), take)
        return k

    def second(j, k):
        b = ((wrap(y + (j >> 1), NY) << 3) + z) * NC + ((j & 1) ^ c)
        count = count_ref[b]
        for r in range(SLOTS):
            n = neg_ref[b, r]
            take = (r < count) & ((n >> 4) == y) & ((n & 1) == c)
            k = push(k, wrap((n >> 1) - z, NZ), j, take)
        return k

    n1 = lax.fori_loop(0, NZ, first, push(0, 0, 0, jnp.bool_(True)))
    n2 = lax.fori_loop(0, NY * NC, second, push(n1, 0, 0, jnp.bool_(True)))
    for i, v in enumerate((n1, n2, x, y, z, c)):
        ent_ref[2, i] = v


def build_list(neg_blocks, neg_count):
    return pl.pallas_call(
        list_kernel,
        out_shape=jax.ShapeDtypeStruct((3, LIST_LEN), jnp.int32),
        in_specs=[spec_s(), spec_s()],
        out_specs=spec_s(),
        name="block_list",
    )(neg_blocks, neg_count)


NQ, NCODE = 9, 8


def fill_blocks(q_refs, c_refs, qs, cs):
    own, l1, l2, l3, r1, r2, r3, r4, l4 = q_refs
    for e, ref in ((0, own), (1, l1), (2, l2), (3, l3), (7, r1), (6, r2), (5, r3)):
        qs[e] = ref[...]
    qs[4, :HALF] = r4[...]
    qs[4, HALF:] = l4[...]
    for j, ref in enumerate(c_refs):
        cs[j] = ref[...]


def dot_nt(a, b):
    return lax.dot_general(a, b, (((1,), (1,)), ((), ())), preferred_element_type=F32)


def dot_nn(a, b):
    return lax.dot_general(a, b, (((1,), (0,)), ((), ())), preferred_element_type=F32)


def dot_tn(a, b):
    return lax.dot_general(a, b, (((0,), (0,)), ((), ())), preferred_element_type=F32)


def quarter_starts(x):
    return [pl.multiple_of(wrap(x + d, NX) * QUARTER, QUARTER) for d in range(NX)]


def score_kernel(ent, *refs):
    q_refs, c_refs = refs[:NQ], refs[NQ : NQ + NCODE]
    outs = refs[NQ + NCODE : NQ + NCODE + NX]
    qs, cs, tile = refs[NQ + NCODE + NX :]
    fill_blocks(q_refs, c_refs, qs, cs)
    n1, n2 = ent[2, 0], ent[2, 1]
    starts = quarter_starts(ent[2, 2])

    def emit(k, s):
        tile[...] = s
        for out, start in zip(outs, starts):
            out[k] = tile[pl.ds(start, QUARTER), :]

    def first(k, _):
        emit(k, dot_nt(qs[ent[0, k]], cs[ent[1, k]]))
        return 0

    def second(k, _):
        emit(k, dot_nt(cs[ent[1, k]], qs[ent[0, k]]))
        return 0

    lax.fori_loop(0, n1, first, 0)
    lax.fori_loop(n1, n2, second, 0)


def partial_scores(cap, ent, q_parts, c_parts):
    feats = q_parts[0].shape[-1]
    return pl.pallas_call(
        score_kernel,
        out_shape=[jax.ShapeDtypeStruct((cap, QUARTER, BLK), F32)] * NX,
        in_specs=[spec_s()] + [spec_v()] * (NQ + NCODE),
        out_specs=[spec_v()] * NX,
        scratch_shapes=[
            VMEM((NZ, BLK, feats), BF16),
            VMEM((NY * NC, BLK, feats), BF16),
            VMEM((BLK, BLK), F32),
        ],
        compiler_params=pltpu.CompilerParams(vmem_limit_bytes=40 * 2**20),
        name="scores",
    )(ent, *q_parts, *c_parts)


def group_lane(ent, k, n1):
    y, z, c = ent[2, 3], ent[2, 4], ent[2, 5]
    e, j = ent[0, k], ent[1, k]
    first = wrap(z + e, NZ)
    second = NZ + 2 * wrap(y + (j >> 1), NY) + ((j & 1) ^ c)
    return jnp.where(k < n1, first, second)


def lanes_of(rows):
    return lax.broadcasted_iota(jnp.int32, (rows, BLK), 1)


def stats_kernel(ent, s0, s1, s2, s3, s_ref, st_ref, top, tot):
    n1, n2 = ent[2, 0], ent[2, 1]
    top[...] = jnp.full(top.shape, LOWEST, F32)
    tot[...] = jnp.zeros(tot.shape, F32)

    def first(k, _):
        s = INV_TEMP * ((s0[k] + s2[k]) + (s1[k] + s3[k]))
        s_ref[k] = s
        g = group_lane(ent, k, n1)
        top[g] = jnp.maximum(top[g], s)
        return 0

    lax.fori_loop(0, n2, first, 0)
    for g in range(2 * NZ):
        top[g] = jnp.broadcast_to(jnp.max(top[g], axis=1, keepdims=True), (QUARTER, BLK))

    def second(k, _):
        g = group_lane(ent, k, n1)
        tot[g] = tot[g] + jnp.exp(s_ref[k] - top[g])
        return 0

    lax.fori_loop(0, n2, second, 0)
    lane = lanes_of(QUARTER)
    m = jnp.full((QUARTER, BLK), LOWEST, F32)
    l = jnp.zeros((QUARTER, BLK), F32)
    for g in range(2 * NZ):
        m = jnp.where(lane == g, top[g], m)
        l = jnp.where(lane == g, jnp.sum(tot[g], axis=1, keepdims=True), l)
    st_ref[0] = m
    st_ref[1] = l


def local_stats(cap, ent, parts):
    return pl.pallas_call(
        stats_kernel,
        out_shape=[
            jax.ShapeDtypeStruct((cap, QUARTER, BLK), F32),
            jax.ShapeDtypeStruct((2, QUARTER, BLK), F32),
        ],
        in_specs=[spec_s()] + [spec_v()] * NX,
        out_specs=[spec_v()] * 2,
        scratch_shapes=[VMEM((2 * NZ, QUARTER, BLK), F32)] * 2,
        name="local_stats",
    )(ent, *parts)


def grad_kernel(ent, *refs):
    s_refs, st_refs, (prow, pcol) = refs[:NX], refs[NX : 2 * NX], refs[2 * NX : 2 * NX + 2]
    refs = refs[2 * NX + 2 :]
    q_refs, c_refs, refs = refs[:NQ], refs[NQ : NQ + NCODE], refs[NQ + NCODE :]
    own_q, own_c, pq, pc, po = refs[:5]
    qs, cs, acc_q, acc_c, st, tile = refs[5:]
    n1, n2 = ent[2, 0], ent[2, 1]
    fill_blocks(q_refs, c_refs, qs, cs)
    acc_q[...] = jnp.zeros(acc_q.shape, F32)
    acc_c[...] = jnp.zeros(acc_c.shape, F32)
    starts = quarter_starts(ent[2, 2])
    for ref, start in zip(st_refs, starts):
        st[:, pl.ds(start, QUARTER), :] = ref[...]
    lane = lanes_of(BLK)

    def probs(k):
        here = lane == group_lane(ent, k, n1)
        m = jnp.max(jnp.where(here, st[0], LOWEST), axis=1, keepdims=True)
        l = jnp.sum(jnp.where(here, st[1], 0.0), axis=1, keepdims=True)
        for ref, start in zip(s_refs, starts):
            tile[pl.ds(start, QUARTER), :] = ref[k]
        return jnp.exp(tile[...] - m) * (1.0 / l)

    def first(k, hit):
        e, j = ent[0, k], ent[1, k]
        g = (0.5 * (probs(k) - hit)).astype(BF16)
        acc_q[e] += dot_nn(g, cs[j])
        acc_c[j] += dot_tn(g, qs[e])

    def second(k, hit):
        e, j = ent[0, k], ent[1, k]
        g = (0.5 * (probs(k) - hit)).astype(BF16)
        acc_c[j] += dot_nn(g, qs[e])
        acc_q[e] += dot_tn(g, cs[j])

    def far(fn, k, _):
        fn(k, 0.0)
        return 0

    first(0, (pcol[...] == lane).astype(F32))
    lax.fori_loop(1, n1, functools.partial(far, first), 0)
    second(n1, (prow[...] == lax.broadcasted_iota(jnp.int32, (BLK, BLK), 0)).astype(F32))
    lax.fori_loop(n1 + 1, n2, functools.partial(far, second), 0)
    own_q[...] = INV_TEMP * acc_q[0]
    own_c[...] = INV_TEMP * acc_c[0]
    for e in range(1, NZ):
        pq[e - 1] = (INV_TEMP * acc_q[e]).astype(BF16)
    for d in range(NY):
        if d:
            pc[d - 1] = (INV_TEMP * acc_c[2 * d]).astype(BF16)
        po[d] = (INV_TEMP * acc_c[2 * d + 1]).astype(BF16)


def partial_grads(ent, scores, stats, pairing, q_parts, c_parts):
    feats = q_parts[0].shape[-1]
    return pl.pallas_call(
        grad_kernel,
        out_shape=[
            jax.ShapeDtypeStruct((BLK, feats), F32),
            jax.ShapeDtypeStruct((BLK, feats), F32),
            jax.ShapeDtypeStruct((NZ - 1, BLK, feats), BF16),
            jax.ShapeDtypeStruct((NY - 1, BLK, feats), BF16),
            jax.ShapeDtypeStruct((NY, BLK, feats), BF16),
        ],
        in_specs=[spec_s()] + [spec_v()] * (2 * NX + 2 + NQ + NCODE),
        out_specs=[spec_v()] * 5,
        scratch_shapes=[
            VMEM((NZ, BLK, feats), BF16),
            VMEM((NY * NC, BLK, feats), BF16),
            VMEM((NZ, BLK, feats), F32),
            VMEM((NY * NC, BLK, feats), F32),
            VMEM((2, BLK, BLK), F32),
            VMEM((BLK, BLK), F32),
        ],
        compiler_params=pltpu.CompilerParams(vmem_limit_bytes=52 * 2**20),
        name="grads",
    )(ent, *scores, *stats, pairing, pairing.reshape(BLK, 1), *q_parts, *c_parts)


def shift(value, axis, by):
    n = {"x": NX, "y": NY, "z": NZ, "c": NC}[axis]
    return lax.ppermute(value, axis, [(i, (i + by) % n) for i in range(n)])


def merge(a, b):
    m = jnp.maximum(a[0], b[0])
    return jnp.stack([m, a[1] * jnp.exp(a[0] - m) + b[1] * jnp.exp(b[0] - m)])


def merge_over_z(st):
    left, right = shift(st, "z", 1), shift(st, "z", -1)
    two = merge(left, st)
    three = merge(two, right)
    return merge(merge(three, shift(three, "z", 3)), shift(two, "z", -3))


def merge_over_yc(st):
    pair = merge(st, shift(st, "c", 1))
    return merge(
        merge(pair, shift(pair, "y", 2)), merge(shift(pair, "y", 1), shift(pair, "y", -1))
    )


def from_others(value, axis):
    return shift(value, axis, -1), shift(value, axis, 2), shift(value, axis, 1)


def gather_queries(q):
    r1, l1 = shift(q, "z", 1), shift(q, "z", -1)
    r2, l2 = shift(r1, "z", 1), shift(l1, "z", -1)
    r3, l3 = shift(r2, "z", 1), shift(l2, "z", -1)
    r4, l4 = shift(r3[:HALF], "z", 1), shift(l3[HALF:], "z", -1)
    return q, l1, l2, l3, r1, r2, r3, r4, l4


def gather_codes(codes):
    mine = (codes, *from_others(codes, "y"))
    return tuple(v for part in mine for v in (part, shift(part, "c", 1)))


def add(a, b):
    return (a.astype(F32) + b.astype(F32)).astype(BF16)


def reduce_queries(pq):
    r, l = shift(pq[3, :HALF], "z", 1), shift(pq[3, HALF:], "z", -1)
    r = jnp.concatenate([add(r, pq[2, :HALF]), pq[2, HALF:]], axis=0)
    l = jnp.concatenate([pq[4, :HALF], add(l, pq[4, HALF:])], axis=0)
    r, l = add(shift(r, "z", 1), pq[1]), add(shift(l, "z", -1), pq[5])
    r, l = add(shift(r, "z", 1), pq[0]), add(shift(l, "z", -1), pq[6])
    return shift(r, "z", 1), shift(l, "z", -1)


def reduce_codes(pc, po):
    other = shift(po, "c", 1)
    both = add(pc, other[1:])
    return other[0], shift(both[0], "y", 1), shift(both[1], "y", 2), shift(both[2], "y", -1)


def run(cap, queries, codes, pairing, neg_blocks, neg_count):
    ent = build_list(neg_blocks, neg_count)
    with jax.named_scope("gather"):
        c_parts = gather_codes(codes)
        q_parts = gather_queries(queries)
    o0, o1, o2, o3 = partial_scores(cap, ent, q_parts, c_parts)
    with jax.named_scope("scores_over_x"):
        parts = (o0, shift(o1, "x", 1), shift(o2, "x", 2), shift(o3, "x", -1))
    scores, st = local_stats(cap, ent, parts)
    with jax.named_scope("scores_to_x"):
        scores = (scores, *from_others(scores, "x"))
    with jax.named_scope("stats"):
        in_z = lax.broadcasted_iota(jnp.int32, st.shape, 2) < NZ
        st = jnp.where(in_z, merge_over_z(st), merge_over_yc(st))
        stats = (st, *from_others(st, "x"))
    own_q, own_c, pq, pc, po = partial_grads(ent, scores, stats, pairing, q_parts, c_parts)
    with jax.named_scope("reduce"):
        c0, c1, c2, c3 = reduce_codes(pc, po)
        qr, ql = reduce_queries(pq)
    grad_queries = own_q + (qr.astype(F32) + ql.astype(F32))
    grad_codes = own_c + ((c0.astype(F32) + c1.astype(F32)) + (c2.astype(F32) + c3.astype(F32)))
    return grad_queries, grad_codes


def longest_list(neg_blocks, neg_count):
    blocks = neg_blocks.shape[0]
    b = jnp.arange(blocks, dtype=jnp.int32)[:, None]
    live = jnp.arange(SLOTS, dtype=jnp.int32)[None, :] < neg_count[:, None]

    def tile(rows, cols):
        return (((rows >> 4) * NC + (rows & 1)) << 3) + ((cols >> 1) & 7)

    ids = jnp.arange(blocks, dtype=jnp.int32)[:, None, None]
    hits = (tile(b, neg_blocks)[None] == ids).astype(jnp.int32)
    hits += (tile(neg_blocks, b)[None] == ids).astype(jnp.int32)
    return jnp.max(jnp.sum(jnp.where(live[None], hits, 0), axis=(1, 2))) + 2


def local(*args):
    short = run(CAP_SMALL, *args)
    again = (longest_list(*args[3:]) > CAP_SMALL).astype(jnp.int32)
    return lax.while_loop(
        lambda state: state[0] > 0,
        lambda state: (jnp.int32(0), run(CAP_FULL, *args)),
        (again, short),
    )[1]


def solution(mesh):
    grid = Mesh(mesh.devices.reshape(NY, NZ, NC, NX), ("y", "z", "c", "x"))
    in_specs = (P(DP, "x"), P(DP, "x"), P(DP, None), P(), P())
    out_specs = (P(DP, "x"), P(DP, "x"))
    return jax.shard_map(local, mesh=grid, in_specs=in_specs, out_specs=out_specs, check_vma=False)
```

```python
import functools

import jax
import jax.numpy as jnp
from jax import lax
from jax.experimental import pallas as pl
from jax.experimental.pallas import tpu as pltpu
from jax.sharding import Mesh, PartitionSpec as P

INV_TEMP = 50.0
NY, NZ, NC, NX = 4, 8, 2, 4
BLK = 128
SLOTS = 4
QUARTER = BLK // NX
HALF = BLK // 2
CAP_SMALL = 18
CAP_FULL = 80
LOWEST = -3.0e38
DP = ("y", "z", "c")
LIST_LEN = 88
GRANT_PER_SLOT = 5 * 2**14
F32 = jnp.float32
BF16 = jnp.bfloat16
VMEM = pltpu.VMEM
SMEM = pltpu.SMEM


def wrap(v, n):
    return v & (n - 1)


def grant(own, cap):
    return pltpu.CompilerParams(vmem_limit_bytes=own + GRANT_PER_SLOT * cap)


def spec_v():
    return pl.BlockSpec(memory_space=VMEM)


def spec_s():
    return pl.BlockSpec(memory_space=SMEM)


def list_kernel(neg_ref, count_ref, neg_v, count_v, ent_ref, over_ref):
    y, z, c, x = (lax.axis_index(name) for name in ("y", "z", "c", "x"))

    def push(k, e, j, take):
        ent_ref[0, k] = e
        ent_ref[1, k] = j
        return k + take.astype(jnp.int32)

    def first(e, k):
        b = ((y << 3) + wrap(z + e, NZ)) * NC + c
        count = count_ref[b]
        for r in range(SLOTS):
            n = neg_ref[r, b]
            take = (r < count) & (wrap(n >> 1, NZ) == z)
            k = push(k, e, 2 * wrap((n >> 4) - y, NY) + ((n & 1) ^ c), take)
        return k

    def second(j, k):
        b = ((wrap(y + (j >> 1), NY) << 3) + z) * NC + ((j & 1) ^ c)
        count = count_ref[b]
        for r in range(SLOTS):
            n = neg_ref[r, b]
            take = (r < count) & ((n >> 4) == y) & ((n & 1) == c)
            k = push(k, wrap((n >> 1) - z, NZ), j, take)
        return k

    n1 = lax.fori_loop(0, NZ, first, push(0, 0, 0, jnp.bool_(True)))
    n2 = lax.fori_loop(0, NY * NC, second, push(n1, 0, 0, jnp.bool_(True)))
    for i, v in enumerate((n1, n2, x, y, z, c)):
        ent_ref[2, i] = v
    blocks = count_v.shape[1]
    shape = (NZ, blocks)
    group = lax.broadcasted_iota(jnp.int32, shape, 0)
    b = lax.broadcasted_iota(jnp.int32, shape, 1)
    count = jnp.broadcast_to(count_v[...], shape)

    def rows_of(n):
        return ((n >> 4) << 1) + (n & 1)

    def cols_of(n):
        return wrap(n >> 1, NZ)

    def ones(mask):
        return jnp.where(mask, 1.0, 0.0)

    to_cols, to_rows = jnp.zeros(shape, F32), jnp.zeros(shape, F32)
    for r in range(SLOTS):
        n = jnp.broadcast_to(neg_v[pl.ds(r, 1), :], shape)
        to_cols += ones((cols_of(n) == group) & (r < count))
        to_rows += ones((rows_of(n) == group) & (r < count))
    tiles = dot_nt(ones(rows_of(b) == group), to_cols) + dot_nt(to_rows, ones(cols_of(b) == group))
    over_ref[0] = (jnp.max(tiles) + 2.0 > CAP_SMALL).astype(jnp.int32)


def build_list(neg_blocks, neg_count):
    neg = neg_blocks.T
    return pl.pallas_call(
        list_kernel,
        out_shape=[
            jax.ShapeDtypeStruct((3, LIST_LEN), jnp.int32),
            jax.ShapeDtypeStruct((1,), jnp.int32),
        ],
        in_specs=[spec_s(), spec_s(), spec_v(), spec_v()],
        out_specs=[spec_s(), spec_s()],
        compiler_params=grant(2 * 2**20, 0),
        name="block_list",
    )(neg, neg_count, neg, neg_count.reshape(1, -1))


NQ, NCODE = 9, 8


def fill_queries(q_refs, qs):
    own, l1, l2, l3, r1, r2, r3, r4, l4 = q_refs
    for e, ref in ((0, own), (1, l1), (2, l2), (3, l3), (7, r1), (6, r2), (5, r3)):
        qs[e] = ref[...]
    qs[4, :HALF] = r4[...]
    qs[4, HALF:] = l4[...]


def dot_nt(a, b):
    return lax.dot_general(a, b, (((1,), (1,)), ((), ())), preferred_element_type=F32)


def dot_nn(a, b):
    return lax.dot_general(a, b, (((1,), (0,)), ((), ())), preferred_element_type=F32)


def dot_tn(a, b):
    return lax.dot_general(a, b, (((0,), (0,)), ((), ())), preferred_element_type=F32)


def quarter_starts(x):
    return [pl.multiple_of(wrap(x + d, NX) * QUARTER, QUARTER) for d in range(NX)]


def score_kernel(ent, *refs):
    q_refs, c_refs = refs[:NQ], refs[NQ : NQ + NCODE]
    outs = refs[NQ + NCODE : NQ + NCODE + NX]
    qs, cs, tile = refs[NQ + NCODE + NX :]
    fill_queries(q_refs, qs)
    for j, ref in enumerate(c_refs):
        cs[j] = ref[...]
    n1, n2 = ent[2, 0], ent[2, 1]
    starts = quarter_starts(ent[2, 2])

    def emit(k, s):
        tile[...] = s
        for out, start in zip(outs, starts):
            out[k] = tile[pl.ds(start, QUARTER), :]

    def first(k, _):
        emit(k, dot_nt(qs[ent[0, k]], cs[ent[1, k]]))
        return 0

    def second(k, _):
        emit(k, dot_nt(cs[ent[1, k]], qs[ent[0, k]]))
        return 0

    lax.fori_loop(0, n1, first, 0)
    lax.fori_loop(n1, n2, second, 0)


def partial_scores(cap, ent, q_parts, c_parts):
    feats = q_parts[0].shape[-1]
    return pl.pallas_call(
        score_kernel,
        out_shape=[jax.ShapeDtypeStruct((cap, QUARTER, BLK), F32)] * NX,
        in_specs=[spec_s()] + [spec_v()] * (NQ + NCODE),
        out_specs=[spec_v()] * NX,
        scratch_shapes=[
            VMEM((NZ, BLK, feats), BF16),
            VMEM((NY * NC, BLK, feats), BF16),
            VMEM((BLK, BLK), F32),
        ],
        compiler_params=grant(8 * 2**20, cap),
        name="scores",
    )(ent, *q_parts, *c_parts)


def group_lane(ent, k, n1):
    y, z, c = ent[2, 3], ent[2, 4], ent[2, 5]
    e, j = ent[0, k], ent[1, k]
    first = wrap(z + e, NZ)
    second = NZ + 2 * wrap(y + (j >> 1), NY) + ((j & 1) ^ c)
    return jnp.where(k < n1, first, second)


def lanes_of(rows):
    return lax.broadcasted_iota(jnp.int32, (rows, BLK), 1)


def stats_kernel(ent, s0, s1, s2, s3, s_ref, st_ref, top, tot):
    n1, n2 = ent[2, 0], ent[2, 1]
    top[...] = jnp.full(top.shape, LOWEST, F32)
    tot[...] = jnp.zeros(tot.shape, F32)

    def first(k, _):
        s = INV_TEMP * ((s0[k] + s2[k]) + (s1[k] + s3[k]))
        s_ref[k] = s
        g = group_lane(ent, k, n1)
        top[g] = jnp.maximum(top[g], s)
        return 0

    lax.fori_loop(0, n2, first, 0)
    for g in range(2 * NZ):
        top[g] = jnp.broadcast_to(jnp.max(top[g], axis=1, keepdims=True), (QUARTER, BLK))

    def second(k, _):
        g = group_lane(ent, k, n1)
        tot[g] = tot[g] + jnp.exp(s_ref[k] - top[g])
        return 0

    lax.fori_loop(0, n2, second, 0)
    lane = lanes_of(QUARTER)
    m = jnp.full((QUARTER, BLK), LOWEST, F32)
    l = jnp.zeros((QUARTER, BLK), F32)
    for g in range(2 * NZ):
        m = jnp.where(lane == g, top[g], m)
        l = jnp.where(lane == g, jnp.sum(tot[g], axis=1, keepdims=True), l)
    st_ref[0] = m
    st_ref[1] = l


def local_stats(cap, ent, parts):
    return pl.pallas_call(
        stats_kernel,
        out_shape=[
            jax.ShapeDtypeStruct((cap, QUARTER, BLK), F32),
            jax.ShapeDtypeStruct((2, QUARTER, BLK), F32),
        ],
        in_specs=[spec_s()] + [spec_v()] * NX,
        out_specs=[spec_v()] * 2,
        scratch_shapes=[VMEM((2 * NZ, QUARTER, BLK), F32)] * 2,
        compiler_params=grant(2 * 2**20, cap),
        name="local_stats",
    )(ent, *parts)


def query_grad_kernel(ent, *refs):
    s_refs, st_refs, prow = refs[:NX], refs[NX : 2 * NX], refs[2 * NX]
    c_refs, refs = refs[2 * NX + 1 : 2 * NX + 1 + NCODE], refs[2 * NX + 1 + NCODE :]
    g_ref, own, p1, p2, p3, p4a, p4b, m1, m2, m3 = refs[:10]
    cs, acc, st, tile = refs[10:]
    n1, n2 = ent[2, 0], ent[2, 1]
    for j, ref in enumerate(c_refs):
        cs[j] = ref[...]
    acc[...] = jnp.zeros(acc.shape, F32)
    starts = quarter_starts(ent[2, 2])
    for ref, start in zip(st_refs, starts):
        st[:, pl.ds(start, QUARTER), :] = ref[...]
    lane = lanes_of(BLK)

    def coefs(k, hit):
        here = lane == group_lane(ent, k, n1)
        m = jnp.max(jnp.where(here, st[0], LOWEST), axis=1, keepdims=True)
        l = jnp.sum(jnp.where(here, st[1], 0.0), axis=1, keepdims=True)
        for ref, start in zip(s_refs, starts):
            tile[pl.ds(start, QUARTER), :] = ref[k]
        g = (0.5 * (jnp.exp(tile[...] - m) * (1.0 / l) - hit)).astype(BF16)
        g_ref[k] = g
        return g

    def first(k, hit):
        acc[ent[0, k]] += dot_nn(coefs(k, hit), cs[ent[1, k]])

    def second(k, hit):
        acc[ent[0, k]] += dot_tn(coefs(k, hit), cs[ent[1, k]])

    def far(fn, k, _):
        fn(k, 0.0)
        return 0

    hit = (prow[...] == lax.broadcasted_iota(jnp.int32, (BLK, BLK), 0)).astype(F32)
    first(0, hit.T)
    lax.fori_loop(1, n1, functools.partial(far, first), 0)
    second(n1, hit)
    lax.fori_loop(n1 + 1, n2, functools.partial(far, second), 0)
    own[...] = INV_TEMP * acc[0]
    for e, out in ((1, p1), (2, p2), (3, p3), (7, m1), (6, m2), (5, m3)):
        out[...] = (INV_TEMP * acc[e]).astype(BF16)
    p4a[...] = (INV_TEMP * acc[4, :HALF]).astype(BF16)
    p4b[...] = (INV_TEMP * acc[4, HALF:]).astype(BF16)


def query_grads(cap, ent, scores, stats, pairing, c_parts):
    feats = c_parts[0].shape[-1]
    part = jax.ShapeDtypeStruct((BLK, feats), BF16)
    half = jax.ShapeDtypeStruct((HALF, feats), BF16)
    return pl.pallas_call(
        query_grad_kernel,
        out_shape=[
            jax.ShapeDtypeStruct((cap, BLK, BLK), BF16),
            jax.ShapeDtypeStruct((BLK, feats), F32),
            *[part, part, part, half, half, part, part, part],
        ],
        in_specs=[spec_s()] + [spec_v()] * (2 * NX + 1 + NCODE),
        out_specs=[spec_v()] * 10,
        scratch_shapes=[
            VMEM((NY * NC, BLK, feats), BF16),
            VMEM((NZ, BLK, feats), F32),
            VMEM((2, BLK, BLK), F32),
            VMEM((BLK, BLK), F32),
        ],
        compiler_params=grant(10 * 2**20, cap),
        cost_estimate=pl.CostEstimate(flops=10**9, bytes_accessed=12 * 10**6, transcendentals=10**5),
        name="query_grads",
    )(ent, *scores, *stats, pairing, *c_parts)


def code_grad_kernel(ent, g_ref, *refs):
    q_refs, (own, pc1, pc2, pc3, po, qs, acc) = refs[:NQ], refs[NQ:]
    n1, n2 = ent[2, 0], ent[2, 1]
    fill_queries(q_refs, qs)
    acc[...] = jnp.zeros(acc.shape, F32)

    def first(k, _):
        acc[ent[1, k]] += dot_tn(g_ref[k], qs[ent[0, k]])
        return 0

    def second(k, _):
        acc[ent[1, k]] += dot_nn(g_ref[k], qs[ent[0, k]])
        return 0

    lax.fori_loop(0, n1, first, 0)
    lax.fori_loop(n1, n2, second, 0)
    own[...] = INV_TEMP * acc[0]
    for d, out in ((1, pc1), (2, pc2), (3, pc3)):
        out[...] = (INV_TEMP * acc[2 * d]).astype(BF16)
    for d in range(NY):
        po[d] = (INV_TEMP * acc[2 * d + 1]).astype(BF16)


def code_grads(ent, coefs, q_parts):
    feats = q_parts[0].shape[-1]
    part = jax.ShapeDtypeStruct((BLK, feats), BF16)
    return pl.pallas_call(
        code_grad_kernel,
        out_shape=[
            jax.ShapeDtypeStruct((BLK, feats), F32),
            *[part, part, part],
            jax.ShapeDtypeStruct((NY, BLK, feats), BF16),
        ],
        in_specs=[spec_s()] + [spec_v()] * (1 + NQ),
        out_specs=[spec_v()] * 5,
        scratch_shapes=[VMEM((NZ, BLK, feats), BF16), VMEM((NY * NC, BLK, feats), F32)],
        compiler_params=grant(10 * 2**20, coefs.shape[0]),
        cost_estimate=pl.CostEstimate(flops=10**9, bytes_accessed=12 * 10**6, transcendentals=0),
        name="code_grads",
    )(ent, coefs, *q_parts)


def shift(value, axis, by):
    n = {"x": NX, "y": NY, "z": NZ, "c": NC}[axis]
    return lax.ppermute(value, axis, [(i, (i + by) % n) for i in range(n)])


def merge(a, b):
    m = jnp.maximum(a[0], b[0])
    return m, a[1] * jnp.exp(a[0] - m) + b[1] * jnp.exp(b[0] - m)


def small_kernel(fn, name, out_shape, *args):
    def kernel(*refs):
        outs = fn(*(ref[...] for ref in refs[: len(args)]))
        for ref, out in zip(refs[len(args) :], outs):
            ref[...] = out

    return pl.pallas_call(
        kernel,
        out_shape=out_shape,
        in_specs=[spec_v()] * len(args),
        out_specs=[spec_v()] * len(out_shape),
        compiler_params=grant(4 * 2**20, 0),
        name=name,
    )(*args)


def near_stats(st, left, right, other):
    two = merge(left, st)
    return jnp.stack(two), jnp.stack(merge(two, right)), jnp.stack(merge(st, other))


def final_stats(three, pair, z1, z2, y1, y2, y3):
    over_z = merge(merge(three, z1), z2)
    over_yc = merge(merge(pair, y1), merge(y2, y3))
    first = lanes_of(QUARTER) < NZ
    return (jnp.stack([jnp.where(first, a, b) for a, b in zip(over_z, over_yc)]),)


def from_others(value, axis):
    return shift(value, axis, -1), shift(value, axis, 2), shift(value, axis, 1)


def gather(queries, codes, ent):
    r1, l1 = shift(queries, "z", 1), shift(queries, "z", -1)
    c_mine = (codes, *from_others(codes, "y"))
    c_parts = tuple(v for part in c_mine for v in (part, shift(part, "c", 1)))
    r1, l1, ent = lax.optimization_barrier((r1, l1, ent))
    r2, l2 = shift(r1, "z", 1), shift(l1, "z", -1)
    r3, l3 = shift(r2, "z", 1), shift(l2, "z", -1)
    r4, l4 = shift(r3[:HALF], "z", 1), shift(l3[HALF:], "z", -1)
    return (queries, l1, l2, l3, r1, r2, r3, r4, l4), c_parts, ent


def exchange(cap, scores, st):
    others = from_others(scores, "x")
    left, right, other = shift(st, "z", 1), shift(st, "z", -1), shift(st, "c", 1)
    like = jax.ShapeDtypeStruct(st.shape, F32)
    two, three, pair = small_kernel(near_stats, "near_stats", [like] * 3, st, left, right, other)
    z1, z2 = shift(three, "z", 3), shift(two, "z", -3)
    y1, y2, y3 = from_others(pair, "y")
    (st,) = small_kernel(final_stats, "final_stats", [like], three, pair, z1, z2, y1, y2, y3)
    return (scores, *others), (st, *from_others(st, "x"))


def total(*parts):
    out = parts[0].astype(F32)
    for p in parts[1:]:
        out = out + p.astype(F32)
    return out


def join_halves(b, d, r, l):
    r = jnp.concatenate([total(b, r[:HALF]).astype(BF16), r[HALF:]], axis=0)
    return r, jnp.concatenate([l[:HALF], total(d, l[HALF:]).astype(BF16)], axis=0)


def join(a, b, r, l):
    return total(a, r).astype(BF16), total(b, l).astype(BF16)


def join_codes(other, *parts):
    return [total(part, other[d + 1]).astype(BF16) for d, part in enumerate(parts)]


def reduce_queries(p1, p2, p3, p4a, p4b, m1, m2, m3):
    like = [jax.ShapeDtypeStruct(p1.shape, BF16)] * 2
    r, l = shift(p4a, "z", 1), shift(p4b, "z", -1)
    r, l = small_kernel(join_halves, "join_halves", like, r, l, p3, m3)
    for a, b in ((p2, m2), (p1, m1)):
        r, l = shift(r, "z", 1), shift(l, "z", -1)
        r, l = small_kernel(join, "join", like, r, l, a, b)
    return shift(r, "z", 1), shift(l, "z", -1)


def reduce_codes(po, *parts):
    like = [jax.ShapeDtypeStruct(parts[0].shape, BF16)] * 3
    other = shift(po, "c", 1)
    parts = small_kernel(join_codes, "join_codes", like, other, *parts)
    return other[0], *(shift(part, "y", d + 1) for d, part in enumerate(parts))


def run(cap, queries, codes, pairing, neg_blocks, neg_count):
    ent, over = build_list(neg_blocks, neg_count)
    with jax.named_scope("gather"):
        q_parts, c_parts, ent = gather(queries, codes, ent)
    o0, o1, o2, o3 = partial_scores(cap, ent, q_parts, c_parts)
    with jax.named_scope("scores_over_x"):
        parts = (o0, shift(o1, "x", 1), shift(o2, "x", 2), shift(o3, "x", -1))
    scores, st = local_stats(cap, ent, parts)
    with jax.named_scope("stats"):
        scores, stats = exchange(cap, scores, st)
    g, own_q, p1, p2, p3, p4a, p4b, m1, m2, m3 = query_grads(
        cap, ent, scores, stats, pairing, c_parts
    )
    own_c, pc1, pc2, pc3, po = code_grads(ent, g, q_parts)
    with jax.named_scope("reduce"):
        from_z = reduce_queries(p1, p2, p3, p4a, p4b, m1, m2, m3)
        from_yc = reduce_codes(po, pc1, pc2, pc3)
    return over, (total(own_q, *from_z), total(own_c, *from_yc))


def local(*args):
    over, short = run(CAP_SMALL, *args)
    return lax.while_loop(
        lambda state: state[0] > 0,
        lambda state: (jnp.int32(0), run(CAP_FULL, *args)[1]),
        (over[0], short),
    )[1]


def solution(mesh):
    grid = Mesh(mesh.devices.reshape(NY, NZ, NC, NX), ("y", "z", "c", "x"))
    in_specs = (P(DP, "x"), P(DP, "x"), P(DP, None), P(), P())
    out_specs = (P(DP, "x"), P(DP, "x"))
    return jax.shard_map(local, mesh=grid, in_specs=in_specs, out_specs=out_specs, check_vma=False)
```

```python
import functools

import jax
import jax.numpy as jnp
from jax import lax
from jax.experimental import pallas as pl
from jax.experimental.pallas import tpu as pltpu
from jax.sharding import Mesh, PartitionSpec as P

INV_TEMP = 50.0
NY, NZ, NC, NX = 4, 8, 2, 4
BLK = 128
SLOTS = 4
QUARTER = BLK // NX
HALF = BLK // 2
CAP_SMALL = 18
CAP_FULL = 80
LOWEST = -3.0e38
DP = ("y", "z", "c")
LIST_LEN = 88
GRANT_PER_SLOT = 5 * 2**14
F32 = jnp.float32
BF16 = jnp.bfloat16
VMEM = pltpu.VMEM
SMEM = pltpu.SMEM


def wrap(v, n):
    return v & (n - 1)


def grant(own, cap):
    return pltpu.CompilerParams(vmem_limit_bytes=own + GRANT_PER_SLOT * cap)


def spec_v():
    return pl.BlockSpec(memory_space=VMEM)


def spec_s():
    return pl.BlockSpec(memory_space=SMEM)


def list_kernel(neg_ref, count_ref, neg_v, count_v, ent_ref, over_ref):
    y, z, c, x = (lax.axis_index(name) for name in ("y", "z", "c", "x"))

    def push(k, e, j, take):
        ent_ref[0, k] = e
        ent_ref[1, k] = j
        return k + take.astype(jnp.int32)

    def first(e, k):
        b = ((y << 3) + wrap(z + e, NZ)) * NC + c
        count = count_ref[b]
        for r in range(SLOTS):
            n = neg_ref[r, b]
            take = (r < count) & (wrap(n >> 1, NZ) == z)
            k = push(k, e, 2 * wrap((n >> 4) - y, NY) + ((n & 1) ^ c), take)
        return k

    def second(j, k):
        b = ((wrap(y + (j >> 1), NY) << 3) + z) * NC + ((j & 1) ^ c)
        count = count_ref[b]
        for r in range(SLOTS):
            n = neg_ref[r, b]
            take = (r < count) & ((n >> 4) == y) & ((n & 1) == c)
            k = push(k, wrap((n >> 1) - z, NZ), j, take)
        return k

    n1 = lax.fori_loop(0, NZ, first, push(0, 0, 0, jnp.bool_(True)))
    n2 = lax.fori_loop(0, NY * NC, second, push(n1, 0, 0, jnp.bool_(True)))
    for i, v in enumerate((n1, n2, x, y, z, c)):
        ent_ref[2, i] = v
    blocks = count_v.shape[1]
    shape = (NZ, blocks)
    group = lax.broadcasted_iota(jnp.int32, shape, 0)
    b = lax.broadcasted_iota(jnp.int32, shape, 1)
    count = jnp.broadcast_to(count_v[...], shape)

    def rows_of(n):
        return ((n >> 4) << 1) + (n & 1)

    def cols_of(n):
        return wrap(n >> 1, NZ)

    def ones(mask):
        return jnp.where(mask, 1.0, 0.0)

    to_cols, to_rows = jnp.zeros(shape, F32), jnp.zeros(shape, F32)
    for r in range(SLOTS):
        n = jnp.broadcast_to(neg_v[pl.ds(r, 1), :], shape)
        to_cols += ones((cols_of(n) == group) & (r < count))
        to_rows += ones((rows_of(n) == group) & (r < count))
    tiles = dot_nt(ones(rows_of(b) == group), to_cols) + dot_nt(to_rows, ones(cols_of(b) == group))
    over_ref[0] = (jnp.max(tiles) + 2.0 > CAP_SMALL).astype(jnp.int32)


def build_list(neg_blocks, neg_count):
    neg = neg_blocks.T
    return pl.pallas_call(
        list_kernel,
        out_shape=[
            jax.ShapeDtypeStruct((3, LIST_LEN), jnp.int32),
            jax.ShapeDtypeStruct((1,), jnp.int32),
        ],
        in_specs=[spec_s(), spec_s(), spec_v(), spec_v()],
        out_specs=[spec_s(), spec_s()],
        compiler_params=grant(2 * 2**20, 0),
        name="block_list",
    )(neg, neg_count, neg, neg_count.reshape(1, -1))


NQ, NCODE = 9, 8


def fill_queries(q_refs, qs):
    own, l1, l2, l3, r1, r2, r3, r4, l4 = q_refs
    for e, ref in ((0, own), (1, l1), (2, l2), (3, l3), (7, r1), (6, r2), (5, r3)):
        qs[e] = ref[...]
    qs[4, :HALF] = r4[...]
    qs[4, HALF:] = l4[...]


def dot_nt(a, b):
    return lax.dot_general(a, b, (((1,), (1,)), ((), ())), preferred_element_type=F32)


def dot_nn(a, b):
    return lax.dot_general(a, b, (((1,), (0,)), ((), ())), preferred_element_type=F32)


def dot_tn(a, b):
    return lax.dot_general(a, b, (((0,), (0,)), ((), ())), preferred_element_type=F32)


def quarter_starts(x):
    return [pl.multiple_of(wrap(x + d, NX) * QUARTER, QUARTER) for d in range(NX)]


def score_kernel(ent, *refs):
    q_refs, c_refs = refs[:NQ], refs[NQ : NQ + NCODE]
    outs = refs[NQ + NCODE : NQ + NCODE + NX]
    qs, cs, tile = refs[NQ + NCODE + NX :]
    fill_queries(q_refs, qs)
    for j, ref in enumerate(c_refs):
        cs[j] = ref[...]
    n1, n2 = ent[2, 0], ent[2, 1]
    starts = quarter_starts(ent[2, 2])

    def emit(k, s):
        tile[...] = s
        for out, start in zip(outs, starts):
            out[k] = tile[pl.ds(start, QUARTER), :]

    def first(k, _):
        emit(k, dot_nt(qs[ent[0, k]], cs[ent[1, k]]))
        return 0

    def second(k, _):
        emit(k, dot_nt(cs[ent[1, k]], qs[ent[0, k]]))
        return 0

    lax.fori_loop(0, n1, first, 0)
    lax.fori_loop(n1, n2, second, 0)


def partial_scores(cap, ent, q_parts, c_parts):
    feats = q_parts[0].shape[-1]
    return pl.pallas_call(
        score_kernel,
        out_shape=[jax.ShapeDtypeStruct((cap, QUARTER, BLK), F32)] * NX,
        in_specs=[spec_s()] + [spec_v()] * (NQ + NCODE),
        out_specs=[spec_v()] * NX,
        scratch_shapes=[
            VMEM((NZ, BLK, feats), BF16),
            VMEM((NY * NC, BLK, feats), BF16),
            VMEM((BLK, BLK), F32),
        ],
        compiler_params=grant(8 * 2**20, cap),
        name="scores",
    )(ent, *q_parts, *c_parts)


def group_lane(ent, k, n1):
    y, z, c = ent[2, 3], ent[2, 4], ent[2, 5]
    e, j = ent[0, k], ent[1, k]
    first = wrap(z + e, NZ)
    second = NZ + 2 * wrap(y + (j >> 1), NY) + ((j & 1) ^ c)
    return jnp.where(k < n1, first, second)


def lanes_of(rows):
    return lax.broadcasted_iota(jnp.int32, (rows, BLK), 1)


def stats_kernel(ent, s0, s1, s2, s3, s_ref, st_ref, top, tot):
    n1, n2 = ent[2, 0], ent[2, 1]
    top[...] = jnp.full(top.shape, LOWEST, F32)
    tot[...] = jnp.zeros(tot.shape, F32)

    def first(k, _):
        s = INV_TEMP * ((s0[k] + s2[k]) + (s1[k] + s3[k]))
        s_ref[k] = s
        g = group_lane(ent, k, n1)
        top[g] = jnp.maximum(top[g], s)
        return 0

    lax.fori_loop(0, n2, first, 0)
    for g in range(2 * NZ):
        top[g] = jnp.broadcast_to(jnp.max(top[g], axis=1, keepdims=True), (QUARTER, BLK))

    def second(k, _):
        g = group_lane(ent, k, n1)
        tot[g] = tot[g] + jnp.exp(s_ref[k] - top[g])
        return 0

    lax.fori_loop(0, n2, second, 0)
    lane = lanes_of(QUARTER)
    m = jnp.full((QUARTER, BLK), LOWEST, F32)
    l = jnp.zeros((QUARTER, BLK), F32)
    for g in range(2 * NZ):
        m = jnp.where(lane == g, top[g], m)
        l = jnp.where(lane == g, jnp.sum(tot[g], axis=1, keepdims=True), l)
    st_ref[0] = m
    st_ref[1] = l


def local_stats(cap, ent, parts):
    return pl.pallas_call(
        stats_kernel,
        out_shape=[
            jax.ShapeDtypeStruct((cap, QUARTER, BLK), F32),
            jax.ShapeDtypeStruct((2, QUARTER, BLK), F32),
        ],
        in_specs=[spec_s()] + [spec_v()] * NX,
        out_specs=[spec_v()] * 2,
        scratch_shapes=[VMEM((2 * NZ, QUARTER, BLK), F32)] * 2,
        compiler_params=grant(2 * 2**20, cap),
        name="local_stats",
    )(ent, *parts)


def coef_kernel(ent, s_ref, prow, za, zb, ya, yb, g_ref, top, inv, hits):
    n1, n2 = ent[2, 0], ent[2, 1]
    lane = lanes_of(QUARTER)
    over_z, over_yc = merge(za[...], zb[...]), merge(ya[...], yb[...])
    m, l = (jnp.where(lane < NZ, a, b) for a, b in zip(over_z, over_yc))
    for g in range(2 * NZ):
        here, shape = lane == g, (QUARTER, BLK)
        top[g] = jnp.broadcast_to(jnp.max(jnp.where(here, m, LOWEST), axis=1, keepdims=True), shape)
        inv[g] = jnp.broadcast_to(1.0 / jnp.sum(jnp.where(here, l, 0.0), axis=1, keepdims=True), shape)
    start = pl.multiple_of(ent[2, 2] * QUARTER, QUARTER)
    hit = (prow[...] == lax.broadcasted_iota(jnp.int32, (BLK, BLK), 0)).astype(F32)
    hits[0] = hit.T
    hits[1] = hit

    def probs(k):
        g = group_lane(ent, k, n1)
        return jnp.exp(s_ref[k] - top[g]) * inv[g]

    def far(k, _):
        g_ref[k] = (0.5 * probs(k)).astype(BF16)
        return 0

    lax.fori_loop(1, n1, far, 0)
    lax.fori_loop(n1 + 1, n2, far, 0)
    g_ref[0] = (0.5 * (probs(0) - hits[0, pl.ds(start, QUARTER), :])).astype(BF16)
    g_ref[n1] = (0.5 * (probs(n1) - hits[1, pl.ds(start, QUARTER), :])).astype(BF16)


def coefficients(cap, ent, scores, pairing, *stats):
    return pl.pallas_call(
        coef_kernel,
        out_shape=jax.ShapeDtypeStruct((cap, QUARTER, BLK), BF16),
        in_specs=[spec_s()] + [spec_v()] * 6,
        out_specs=spec_v(),
        scratch_shapes=[
            VMEM((2 * NZ, QUARTER, BLK), F32),
            VMEM((2 * NZ, QUARTER, BLK), F32),
            VMEM((2, BLK, BLK), F32),
        ],
        compiler_params=grant(2 * 2**20, cap),
        name="coefficients",
    )(ent, scores, pairing, *stats)


def query_grad_kernel(ent, *refs):
    quarters, c_refs, refs = refs[:NX], refs[NX : NX + NCODE], refs[NX + NCODE :]
    g_ref, own, p1, p2, p3, p4a, p4b, m1, m2, m3 = refs[:10]
    cs, acc = refs[10:]
    n1, n2 = ent[2, 0], ent[2, 1]
    for j, ref in enumerate(c_refs):
        cs[j] = ref[...]
    acc[...] = jnp.zeros(acc.shape, F32)
    starts = quarter_starts(ent[2, 2])

    def coefs(k):
        for ref, start in zip(quarters, starts):
            g_ref[k, pl.ds(start, QUARTER), :] = ref[k]
        return g_ref[k]

    def first(k, _):
        acc[ent[0, k]] += dot_nn(coefs(k), cs[ent[1, k]])
        return 0

    def second(k, _):
        acc[ent[0, k]] += dot_tn(coefs(k), cs[ent[1, k]])
        return 0

    lax.fori_loop(0, n1, first, 0)
    lax.fori_loop(n1, n2, second, 0)
    own[...] = INV_TEMP * acc[0]
    for e, out in ((1, p1), (2, p2), (3, p3), (7, m1), (6, m2), (5, m3)):
        out[...] = (INV_TEMP * acc[e]).astype(BF16)
    p4a[...] = (INV_TEMP * acc[4, :HALF]).astype(BF16)
    p4b[...] = (INV_TEMP * acc[4, HALF:]).astype(BF16)


def query_grads(cap, ent, coefs, c_parts):
    feats = c_parts[0].shape[-1]
    part = jax.ShapeDtypeStruct((BLK, feats), BF16)
    half = jax.ShapeDtypeStruct((HALF, feats), BF16)
    return pl.pallas_call(
        query_grad_kernel,
        out_shape=[
            jax.ShapeDtypeStruct((cap, BLK, BLK), BF16),
            jax.ShapeDtypeStruct((BLK, feats), F32),
            *[part, part, part, half, half, part, part, part],
        ],
        in_specs=[spec_s()] + [spec_v()] * (NX + NCODE),
        out_specs=[spec_v()] * 10,
        scratch_shapes=[
            VMEM((NY * NC, BLK, feats), BF16),
            VMEM((NZ, BLK, feats), F32),
        ],
        compiler_params=grant(10 * 2**20, cap),
        cost_estimate=pl.CostEstimate(flops=10**9, bytes_accessed=12 * 10**6, transcendentals=0),
        name="query_grads",
    )(ent, *coefs, *c_parts)


def code_grad_kernel(ent, g_ref, *refs):
    q_refs, (own, pc1, pc2, pc3, po, qs, acc) = refs[:NQ], refs[NQ:]
    n1, n2 = ent[2, 0], ent[2, 1]
    fill_queries(q_refs, qs)
    acc[...] = jnp.zeros(acc.shape, F32)

    def first(k, _):
        acc[ent[1, k]] += dot_tn(g_ref[k], qs[ent[0, k]])
        return 0

    def second(k, _):
        acc[ent[1, k]] += dot_nn(g_ref[k], qs[ent[0, k]])
        return 0

    lax.fori_loop(0, n1, first, 0)
    lax.fori_loop(n1, n2, second, 0)
    own[...] = INV_TEMP * acc[0]
    for d, out in ((1, pc1), (2, pc2), (3, pc3)):
        out[...] = (INV_TEMP * acc[2 * d]).astype(BF16)
    for d in range(NY):
        po[d] = (INV_TEMP * acc[2 * d + 1]).astype(BF16)


def code_grads(ent, coefs, q_parts):
    feats = q_parts[0].shape[-1]
    part = jax.ShapeDtypeStruct((BLK, feats), BF16)
    return pl.pallas_call(
        code_grad_kernel,
        out_shape=[
            jax.ShapeDtypeStruct((BLK, feats), F32),
            *[part, part, part],
            jax.ShapeDtypeStruct((NY, BLK, feats), BF16),
        ],
        in_specs=[spec_s()] + [spec_v()] * (1 + NQ),
        out_specs=[spec_v()] * 5,
        scratch_shapes=[VMEM((NZ, BLK, feats), BF16), VMEM((NY * NC, BLK, feats), F32)],
        compiler_params=grant(10 * 2**20, coefs.shape[0]),
        cost_estimate=pl.CostEstimate(flops=10**9, bytes_accessed=12 * 10**6, transcendentals=0),
        name="code_grads",
    )(ent, coefs, *q_parts)


def shift(value, axis, by):
    n = {"x": NX, "y": NY, "z": NZ, "c": NC}[axis]
    return lax.ppermute(value, axis, [(i, (i + by) % n) for i in range(n)])


def merge(a, b):
    m = jnp.maximum(a[0], b[0])
    return m, a[1] * jnp.exp(a[0] - m) + b[1] * jnp.exp(b[0] - m)


def small_kernel(fn, name, out_shape, *args):
    def kernel(*refs):
        outs = fn(*(ref[...] for ref in refs[: len(args)]))
        for ref, out in zip(refs[len(args) :], outs):
            ref[...] = out

    return pl.pallas_call(
        kernel,
        out_shape=out_shape,
        in_specs=[spec_v()] * len(args),
        out_specs=[spec_v()] * len(out_shape),
        compiler_params=grant(4 * 2**20, 0),
        name=name,
    )(*args)


def merge_both(za, zb, ya, yb):
    return jnp.stack(merge(za, zb)), jnp.stack(merge(ya, yb))


def swap(value, axis, bit):
    n = {"y": NY, "z": NZ, "c": NC}[axis]
    return lax.ppermute(value, axis, [(i, i ^ bit) for i in range(n)])


def exchange(st):
    like = [jax.ShapeDtypeStruct(st.shape, F32)] * 2
    over_z, over_yc = st, st
    for z_bit, (axis, bit) in ((1, ("c", 1)), (2, ("y", 1))):
        over_z, over_yc = small_kernel(
            merge_both, "merge", like, over_z, swap(over_z, "z", z_bit), over_yc, swap(over_yc, axis, bit)
        )
    return over_z, swap(over_z, "z", 4), over_yc, swap(over_yc, "y", 2)


def from_others(value, axis):
    return shift(value, axis, -1), shift(value, axis, 2), shift(value, axis, 1)


def gather(queries, codes, ent):
    r1, l1 = shift(queries, "z", 1), shift(queries, "z", -1)
    c_mine = (codes, *from_others(codes, "y"))
    c_parts = tuple(v for part in c_mine for v in (part, shift(part, "c", 1)))
    r1, l1, ent = lax.optimization_barrier((r1, l1, ent))
    r2, l2 = shift(r1, "z", 1), shift(l1, "z", -1)
    r3, l3 = shift(r2, "z", 1), shift(l2, "z", -1)
    r4, l4 = shift(r3[:HALF], "z", 1), shift(l3[HALF:], "z", -1)
    return (queries, l1, l2, l3, r1, r2, r3, r4, l4), c_parts, ent


def total(*parts):
    out = parts[0].astype(F32)
    for p in parts[1:]:
        out = out + p.astype(F32)
    return out


def join_halves(b, d, r, l):
    r = jnp.concatenate([total(b, r[:HALF]).astype(BF16), r[HALF:]], axis=0)
    return r, jnp.concatenate([l[:HALF], total(d, l[HALF:]).astype(BF16)], axis=0)


def join(a, b, r, l):
    return total(a, r).astype(BF16), total(b, l).astype(BF16)


def join_codes(other, *parts):
    return [total(part, other[d + 1]).astype(BF16) for d, part in enumerate(parts)]


def reduce_queries(g, p1, p2, p3, p4a, p4b, m1, m2, m3):
    like = [jax.ShapeDtypeStruct(p1.shape, BF16)] * 2
    r, l = shift(p4a, "z", 1), shift(p4b, "z", -1)
    r, l = small_kernel(join_halves, "join_halves", like, r, l, p3, m3)
    for a, b in ((p2, m2), (p1, m1)):
        r, l = shift(r, "z", 1), shift(l, "z", -1)
        r, l = small_kernel(join, "join", like, r, l, a, b)
    return (shift(r, "z", 1), shift(l, "z", -1)), g


def reduce_codes(po, *parts):
    like = [jax.ShapeDtypeStruct(parts[0].shape, BF16)] * 3
    other = shift(po, "c", 1)
    parts = small_kernel(join_codes, "join_codes", like, other, *parts)
    return other[0], *(shift(part, "y", d + 1) for d, part in enumerate(parts))


def run(cap, queries, codes, pairing, neg_blocks, neg_count):
    ent, over = build_list(neg_blocks, neg_count)
    with jax.named_scope("gather"):
        q_parts, c_parts, ent = gather(queries, codes, ent)
    o0, o1, o2, o3 = partial_scores(cap, ent, q_parts, c_parts)
    with jax.named_scope("scores_over_x"):
        parts = (o0, shift(o1, "x", 1), shift(o2, "x", 2), shift(o3, "x", -1))
    scores, st = local_stats(cap, ent, parts)
    with jax.named_scope("stats"):
        stats = exchange(st)
    coefs = coefficients(cap, ent, scores, pairing, *stats)
    with jax.named_scope("coefs_over_x"):
        coefs = (coefs, *from_others(coefs, "x"))
    g, own_q, *parts = query_grads(cap, ent, coefs, c_parts)
    with jax.named_scope("reduce"):
        from_z, g = reduce_queries(g, *parts)
        own_c, pc1, pc2, pc3, po = code_grads(ent, g, q_parts)
        from_yc = reduce_codes(po, pc1, pc2, pc3)
    return over, (total(own_q, *from_z), total(own_c, *from_yc))


def local(*args):
    over, short = run(CAP_SMALL, *args)
    return lax.while_loop(
        lambda state: state[0] > 0,
        lambda state: (jnp.int32(0), run(CAP_FULL, *args)[1]),
        (over[0], short),
    )[1]


def solution(mesh):
    grid = Mesh(mesh.devices.reshape(NY, NZ, NC, NX), ("y", "z", "c", "x"))
    in_specs = (P(DP, "x"), P(DP, "x"), P(DP, None), P(), P())
    out_specs = (P(DP, "x"), P(DP, "x"))
    return jax.shard_map(local, mesh=grid, in_specs=in_specs, out_specs=out_specs, check_vma=False)
```

```python
import functools

import jax
import jax.numpy as jnp
from jax import lax
from jax.experimental import pallas as pl
from jax.experimental.pallas import tpu as pltpu
from jax.sharding import Mesh, PartitionSpec as P

INV_TEMP = 50.0
NY, NZ, NC, NX = 4, 8, 2, 4
BLK = 128
SLOTS = 4
QUARTER = BLK // NX
HALF = BLK // 2
CAP_SMALL = 18
CAP_FULL = 80
LOWEST = -3.0e38
DP = ("y", "z", "c")
LIST_LEN = 88
GRANT_PER_SLOT = 5 * 2**14
F32 = jnp.float32
BF16 = jnp.bfloat16
VMEM = pltpu.VMEM
SMEM = pltpu.SMEM


def wrap(v, n):
    return v & (n - 1)


def grant(own, cap):
    return pltpu.CompilerParams(vmem_limit_bytes=own + GRANT_PER_SLOT * cap)


def spec_v():
    return pl.BlockSpec(memory_space=VMEM)


def spec_s():
    return pl.BlockSpec(memory_space=SMEM)


def list_kernel(neg_ref, count_ref, neg_v, count_v, ent_ref, over_ref):
    y, z, c, x = (lax.axis_index(name) for name in ("y", "z", "c", "x"))

    def push(k, e, j, take):
        ent_ref[0, k] = e
        ent_ref[1, k] = j
        return k + take.astype(jnp.int32)

    def first(e, k):
        b = ((y << 3) + wrap(z + e, NZ)) * NC + c
        count = count_ref[b]
        for r in range(SLOTS):
            n = neg_ref[r, b]
            take = (r < count) & (wrap(n >> 1, NZ) == z)
            k = push(k, e, 2 * wrap((n >> 4) - y, NY) + ((n & 1) ^ c), take)
        return k

    def second(j, k):
        b = ((wrap(y + (j >> 1), NY) << 3) + z) * NC + ((j & 1) ^ c)
        count = count_ref[b]
        for r in range(SLOTS):
            n = neg_ref[r, b]
            take = (r < count) & ((n >> 4) == y) & ((n & 1) == c)
            k = push(k, wrap((n >> 1) - z, NZ), j, take)
        return k

    n1 = lax.fori_loop(0, NZ, first, push(0, 0, 0, jnp.bool_(True)))
    n2 = lax.fori_loop(0, NY * NC, second, push(n1, 0, 0, jnp.bool_(True)))
    for i, v in enumerate((n1, n2, x, y, z, c)):
        ent_ref[2, i] = v
    blocks = count_v.shape[1]
    shape = (NZ, blocks)
    group = lax.broadcasted_iota(jnp.int32, shape, 0)
    b = lax.broadcasted_iota(jnp.int32, shape, 1)
    count = jnp.broadcast_to(count_v[...], shape)

    def rows_of(n):
        return ((n >> 4) << 1) + (n & 1)

    def cols_of(n):
        return wrap(n >> 1, NZ)

    def ones(mask):
        return jnp.where(mask, 1.0, 0.0)

    to_cols, to_rows = jnp.zeros(shape, F32), jnp.zeros(shape, F32)
    for r in range(SLOTS):
        n = jnp.broadcast_to(neg_v[pl.ds(r, 1), :], shape)
        to_cols += ones((cols_of(n) == group) & (r < count))
        to_rows += ones((rows_of(n) == group) & (r < count))
    tiles = dot_nt(ones(rows_of(b) == group), to_cols) + dot_nt(to_rows, ones(cols_of(b) == group))
    over_ref[0] = (jnp.max(tiles) + 2.0 > CAP_SMALL).astype(jnp.int32)


def build_list(neg_blocks, neg_count):
    neg = neg_blocks.T
    return pl.pallas_call(
        list_kernel,
        out_shape=[
            jax.ShapeDtypeStruct((3, LIST_LEN), jnp.int32),
            jax.ShapeDtypeStruct((1,), jnp.int32),
        ],
        in_specs=[spec_s(), spec_s(), spec_v(), spec_v()],
        out_specs=[spec_s(), spec_s()],
        compiler_params=grant(2 * 2**20, 0),
        name="block_list",
    )(neg, neg_count, neg, neg_count.reshape(1, -1))


NQ, NCODE = 9, 8


def fill_queries(q_refs, qs):
    own, l1, l2, l3, r1, r2, r3, r4, l4 = q_refs
    for e, ref in ((0, own), (1, l1), (2, l2), (3, l3), (7, r1), (6, r2), (5, r3)):
        qs[e] = ref[...]
    qs[4, :HALF] = r4[...]
    qs[4, HALF:] = l4[...]


def dot_nt(a, b):
    return lax.dot_general(a, b, (((1,), (1,)), ((), ())), preferred_element_type=F32)


def dot_nn(a, b):
    return lax.dot_general(a, b, (((1,), (0,)), ((), ())), preferred_element_type=F32)


def dot_tn(a, b):
    return lax.dot_general(a, b, (((0,), (0,)), ((), ())), preferred_element_type=F32)


def quarter_starts(x):
    return [pl.multiple_of(wrap(x + d, NX) * QUARTER, QUARTER) for d in range(NX)]


def score_kernel(ent, *refs):
    q_refs, c_refs = refs[:NQ], refs[NQ : NQ + NCODE]
    outs = refs[NQ + NCODE : NQ + NCODE + NX]
    qs, cs, tile = refs[NQ + NCODE + NX :]
    fill_queries(q_refs, qs)
    for j, ref in enumerate(c_refs):
        cs[j] = ref[...]
    n1, n2 = ent[2, 0], ent[2, 1]
    starts = quarter_starts(ent[2, 2])

    def emit(k, s):
        tile[...] = s
        for out, start in zip(outs, starts):
            out[k] = tile[pl.ds(start, QUARTER), :]

    def first(k, _):
        emit(k, dot_nt(qs[ent[0, k]], cs[ent[1, k]]))
        return 0

    def second(k, _):
        emit(k, dot_nt(cs[ent[1, k]], qs[ent[0, k]]))
        return 0

    lax.fori_loop(0, n1, first, 0)
    lax.fori_loop(n1, n2, second, 0)


def partial_scores(cap, ent, q_parts, c_parts):
    feats = q_parts[0].shape[-1]
    return pl.pallas_call(
        score_kernel,
        out_shape=[jax.ShapeDtypeStruct((cap, QUARTER, BLK), F32)] * NX,
        in_specs=[spec_s()] + [spec_v()] * (NQ + NCODE),
        out_specs=[spec_v()] * NX,
        scratch_shapes=[
            VMEM((NZ, BLK, feats), BF16),
            VMEM((NY * NC, BLK, feats), BF16),
            VMEM((BLK, BLK), F32),
        ],
        compiler_params=grant(8 * 2**20, cap),
        name="scores",
    )(ent, *q_parts, *c_parts)


def group_lane(ent, k, n1):
    y, z, c = ent[2, 3], ent[2, 4], ent[2, 5]
    e, j = ent[0, k], ent[1, k]
    first = wrap(z + e, NZ)
    second = NZ + 2 * wrap(y + (j >> 1), NY) + ((j & 1) ^ c)
    return jnp.where(k < n1, first, second)


def lanes_of(rows):
    return lax.broadcasted_iota(jnp.int32, (rows, BLK), 1)


def stats_kernel(ent, s0, s1, s2, s3, s_ref, st_ref, top, tot):
    n1, n2 = ent[2, 0], ent[2, 1]
    top[...] = jnp.full(top.shape, LOWEST, F32)
    tot[...] = jnp.zeros(tot.shape, F32)

    def first(k, _):
        s = INV_TEMP * ((s0[k] + s2[k]) + (s1[k] + s3[k]))
        s_ref[k] = s
        g = group_lane(ent, k, n1)
        top[g] = jnp.maximum(top[g], s)
        return 0

    lax.fori_loop(0, n2, first, 0)
    for g in range(2 * NZ):
        top[g] = jnp.broadcast_to(jnp.max(top[g], axis=1, keepdims=True), (QUARTER, BLK))

    def second(k, _):
        g = group_lane(ent, k, n1)
        tot[g] = tot[g] + jnp.exp(s_ref[k] - top[g])
        return 0

    lax.fori_loop(0, n2, second, 0)
    lane = lanes_of(QUARTER)
    m = jnp.full((QUARTER, BLK), LOWEST, F32)
    l = jnp.zeros((QUARTER, BLK), F32)
    for g in range(2 * NZ):
        m = jnp.where(lane == g, top[g], m)
        l = jnp.where(lane == g, jnp.sum(tot[g], axis=1, keepdims=True), l)
    st_ref[0] = m
    st_ref[1] = l


def local_stats(cap, ent, parts):
    return pl.pallas_call(
        stats_kernel,
        out_shape=[
            jax.ShapeDtypeStruct((cap, QUARTER, BLK), F32),
            jax.ShapeDtypeStruct((2, QUARTER, BLK), F32),
        ],
        in_specs=[spec_s()] + [spec_v()] * NX,
        out_specs=[spec_v()] * 2,
        scratch_shapes=[VMEM((2 * NZ, QUARTER, BLK), F32)] * 2,
        compiler_params=grant(2 * 2**20, cap),
        name="local_stats",
    )(ent, *parts)


def coef_kernel(ent, s_ref, prow, za, zb, ya, yb, g_ref, top, inv, hits):
    n1, n2 = ent[2, 0], ent[2, 1]
    lane = lanes_of(QUARTER)
    over_z, over_yc = merge(za[...], zb[...]), merge(ya[...], yb[...])
    m, l = (jnp.where(lane < NZ, a, b) for a, b in zip(over_z, over_yc))
    for g in range(2 * NZ):
        here, shape = lane == g, (QUARTER, BLK)
        top[g] = jnp.broadcast_to(jnp.max(jnp.where(here, m, LOWEST), axis=1, keepdims=True), shape)
        inv[g] = jnp.broadcast_to(1.0 / jnp.sum(jnp.where(here, l, 0.0), axis=1, keepdims=True), shape)
    start = pl.multiple_of(ent[2, 2] * QUARTER, QUARTER)
    hit = (prow[...] == lax.broadcasted_iota(jnp.int32, (BLK, BLK), 0)).astype(F32)
    hits[0] = hit.T
    hits[1] = hit

    def probs(k):
        g = group_lane(ent, k, n1)
        return jnp.exp(s_ref[k] - top[g]) * inv[g]

    def far(k, _):
        g_ref[k] = (0.5 * probs(k)).astype(BF16)
        return 0

    lax.fori_loop(1, n1, far, 0)
    lax.fori_loop(n1 + 1, n2, far, 0)
    g_ref[0] = (0.5 * (probs(0) - hits[0, pl.ds(start, QUARTER), :])).astype(BF16)
    g_ref[n1] = (0.5 * (probs(n1) - hits[1, pl.ds(start, QUARTER), :])).astype(BF16)


def coefficients(cap, ent, scores, pairing, *stats):
    return pl.pallas_call(
        coef_kernel,
        out_shape=jax.ShapeDtypeStruct((cap, QUARTER, BLK), BF16),
        in_specs=[spec_s()] + [spec_v()] * 6,
        out_specs=spec_v(),
        scratch_shapes=[
            VMEM((2 * NZ, QUARTER, BLK), F32),
            VMEM((2 * NZ, QUARTER, BLK), F32),
            VMEM((2, BLK, BLK), F32),
        ],
        compiler_params=grant(2 * 2**20, cap),
        name="coefficients",
    )(ent, scores, pairing, *stats)


def query_grad_kernel(ent, *refs):
    quarters, c_refs, refs = refs[:NX], refs[NX : NX + NCODE], refs[NX + NCODE :]
    g_ref, own, p1, p2, p3, p4a, p4b, m1, m2, m3 = refs[:10]
    cs, acc = refs[10:]
    n1, n2 = ent[2, 0], ent[2, 1]
    for j, ref in enumerate(c_refs):
        cs[j] = ref[...]
    acc[...] = jnp.zeros(acc.shape, F32)
    starts = quarter_starts(ent[2, 2])

    def coefs(k):
        for ref, start in zip(quarters, starts):
            g_ref[k, pl.ds(start, QUARTER), :] = ref[k]
        return g_ref[k]

    def first(k, _):
        acc[ent[0, k]] += dot_nn(coefs(k), cs[ent[1, k]])
        return 0

    def second(k, _):
        acc[ent[0, k]] += dot_tn(coefs(k), cs[ent[1, k]])
        return 0

    lax.fori_loop(0, n1, first, 0)
    lax.fori_loop(n1, n2, second, 0)
    own[...] = INV_TEMP * acc[0]
    for e, out in ((1, p1), (2, p2), (3, p3), (7, m1), (6, m2), (5, m3)):
        out[...] = (INV_TEMP * acc[e]).astype(BF16)
    p4a[...] = (INV_TEMP * acc[4, :HALF]).astype(BF16)
    p4b[...] = (INV_TEMP * acc[4, HALF:]).astype(BF16)


def query_grads(cap, ent, coefs, c_parts):
    feats = c_parts[0].shape[-1]
    part = jax.ShapeDtypeStruct((BLK, feats), BF16)
    half = jax.ShapeDtypeStruct((HALF, feats), BF16)
    return pl.pallas_call(
        query_grad_kernel,
        out_shape=[
            jax.ShapeDtypeStruct((cap, BLK, BLK), BF16),
            jax.ShapeDtypeStruct((BLK, feats), F32),
            *[part, part, part, half, half, part, part, part],
        ],
        in_specs=[spec_s()] + [spec_v()] * (NX + NCODE),
        out_specs=[spec_v()] * 10,
        scratch_shapes=[
            VMEM((NY * NC, BLK, feats), BF16),
            VMEM((NZ, BLK, feats), F32),
        ],
        compiler_params=grant(10 * 2**20, cap),
        cost_estimate=pl.CostEstimate(flops=10**9, bytes_accessed=12 * 10**6, transcendentals=0),
        name="query_grads",
    )(ent, *coefs, *c_parts)


def code_grad_kernel(ent, g_ref, *refs):
    q_refs, (own, pc1, pc2, pc3, po, qs, acc) = refs[:NQ], refs[NQ:]
    n1, n2 = ent[2, 0], ent[2, 1]
    fill_queries(q_refs, qs)
    acc[...] = jnp.zeros(acc.shape, F32)

    def first(k, _):
        acc[ent[1, k]] += dot_tn(g_ref[k], qs[ent[0, k]])
        return 0

    def second(k, _):
        acc[ent[1, k]] += dot_nn(g_ref[k], qs[ent[0, k]])
        return 0

    lax.fori_loop(0, n1, first, 0)
    lax.fori_loop(n1, n2, second, 0)
    own[...] = INV_TEMP * acc[0]
    for d, out in ((1, pc1), (2, pc2), (3, pc3)):
        out[...] = (INV_TEMP * acc[2 * d]).astype(BF16)
    for d in range(NY):
        po[d] = (INV_TEMP * acc[2 * d + 1]).astype(BF16)


def code_grads(ent, coefs, q_parts):
    feats = q_parts[0].shape[-1]
    part = jax.ShapeDtypeStruct((BLK, feats), BF16)
    return pl.pallas_call(
        code_grad_kernel,
        out_shape=[
            jax.ShapeDtypeStruct((BLK, feats), F32),
            *[part, part, part],
            jax.ShapeDtypeStruct((NY, BLK, feats), BF16),
        ],
        in_specs=[spec_s()] + [spec_v()] * (1 + NQ),
        out_specs=[spec_v()] * 5,
        scratch_shapes=[VMEM((NZ, BLK, feats), BF16), VMEM((NY * NC, BLK, feats), F32)],
        compiler_params=grant(10 * 2**20, coefs.shape[0]),
        cost_estimate=pl.CostEstimate(flops=10**9, bytes_accessed=12 * 10**6, transcendentals=0),
        name="code_grads",
    )(ent, coefs, *q_parts)


def shift(value, axis, by):
    n = {"x": NX, "y": NY, "z": NZ, "c": NC}[axis]
    return lax.ppermute(value, axis, [(i, (i + by) % n) for i in range(n)])


def merge(a, b):
    m = jnp.maximum(a[0], b[0])
    return m, a[1] * jnp.exp(a[0] - m) + b[1] * jnp.exp(b[0] - m)


def small_kernel(fn, name, out_shape, *args):
    def kernel(*refs):
        outs = fn(*(ref[...] for ref in refs[: len(args)]))
        for ref, out in zip(refs[len(args) :], outs):
            ref[...] = out

    return pl.pallas_call(
        kernel,
        out_shape=out_shape,
        in_specs=[spec_v()] * len(args),
        out_specs=[spec_v()] * len(out_shape),
        compiler_params=grant(4 * 2**20, 0),
        name=name,
    )(*args)


def merge_both(za, zb, ya, yb):
    return jnp.stack(merge(za, zb)), jnp.stack(merge(ya, yb))


def swap(value, axis, bit):
    n = {"y": NY, "z": NZ, "c": NC}[axis]
    return lax.ppermute(value, axis, [(i, i ^ bit) for i in range(n)])


def exchange(st):
    like = [jax.ShapeDtypeStruct(st.shape, F32)] * 2
    over_z, over_yc = st, st
    for z_bit, (axis, bit) in ((1, ("c", 1)), (2, ("y", 1))):
        over_z, over_yc = small_kernel(
            merge_both, "merge", like, over_z, swap(over_z, "z", z_bit), over_yc, swap(over_yc, axis, bit)
        )
    return over_z, swap(over_z, "z", 4), over_yc, swap(over_yc, "y", 2)


def from_others(value, axis):
    return shift(value, axis, -1), shift(value, axis, 2), shift(value, axis, 1)


def gather(queries, codes, ent):
    r1, l1 = shift(queries, "z", 1), shift(queries, "z", -1)
    c_mine = (codes, *from_others(codes, "y"))
    c_parts = tuple(v for part in c_mine for v in (part, shift(part, "c", 1)))
    r1, l1, ent = lax.optimization_barrier((r1, l1, ent))
    r2, l2 = shift(r1, "z", 1), shift(l1, "z", -1)
    r3, l3 = shift(r2, "z", 1), shift(l2, "z", -1)
    r4, l4 = shift(r3[:HALF], "z", 1), shift(l3[HALF:], "z", -1)
    return (queries, l1, l2, l3, r1, r2, r3, r4, l4), c_parts, ent


def total(*parts):
    out = parts[0].astype(F32)
    for p in parts[1:]:
        out = out + p.astype(F32)
    return out


def join_halves(b, d, r, l):
    r = jnp.concatenate([total(b, r[:HALF]).astype(BF16), r[HALF:]], axis=0)
    return r, jnp.concatenate([l[:HALF], total(d, l[HALF:]).astype(BF16)], axis=0)


def join(a, b, r, l):
    return total(a, r).astype(BF16), total(b, l).astype(BF16)


def join_codes(other, *parts):
    return [total(part, other[d + 1]).astype(BF16) for d, part in enumerate(parts)]


def reduce_queries(g, p1, p2, p3, p4a, p4b, m1, m2, m3):
    like = [jax.ShapeDtypeStruct(p1.shape, BF16)] * 2
    r, l = shift(p4a, "z", 1), shift(p4b, "z", -1)
    r, l = small_kernel(join_halves, "join_halves", like, r, l, p3, m3)
    for a, b in ((p2, m2), (p1, m1)):
        r, l = shift(r, "z", 1), shift(l, "z", -1)
        r, l = small_kernel(join, "join", like, r, l, a, b)
    return (shift(r, "z", 1), shift(l, "z", -1)), g


def reduce_codes(po, *parts):
    like = [jax.ShapeDtypeStruct(parts[0].shape, BF16)] * 3
    other = shift(po, "c", 1)
    parts = small_kernel(join_codes, "join_codes", like, other, *parts)
    return other[0], *(shift(part, "y", d + 1) for d, part in enumerate(parts))


def run(cap, queries, codes, pairing, neg_blocks, neg_count):
    ent, over = build_list(neg_blocks, neg_count)
    with jax.named_scope("gather"):
        q_parts, c_parts, ent = gather(queries, codes, ent)
    o0, o1, o2, o3 = partial_scores(cap, ent, q_parts, c_parts)
    with jax.named_scope("scores_over_x"):
        parts = (o0, shift(o1, "x", 1), shift(o2, "x", 2), shift(o3, "x", -1))
    scores, st = local_stats(cap, ent, parts)
    with jax.named_scope("stats"):
        stats = exchange(st)
    coefs = coefficients(cap, ent, scores, pairing, *stats)
    with jax.named_scope("coefs_over_x"):
        coefs = (coefs, *from_others(coefs, "x"))
    g, own_q, *parts = query_grads(cap, ent, coefs, c_parts)
    with jax.named_scope("reduce"):
        from_z, g = reduce_queries(g, *parts)
        own_c, pc1, pc2, pc3, po = code_grads(ent, g, q_parts)
        from_yc = reduce_codes(po, pc1, pc2, pc3)
    return over, (total(own_q, *from_z), total(own_c, *from_yc))


def long_query_grad_kernel(ent, *refs):
    s_refs, st_refs, prow = refs[:NX], refs[NX : 2 * NX], refs[2 * NX]
    c_refs, refs = refs[2 * NX + 1 : 2 * NX + 1 + NCODE], refs[2 * NX + 1 + NCODE :]
    g_ref, own, p1, p2, p3, p4a, p4b, m1, m2, m3 = refs[:10]
    cs, acc, st, tile = refs[10:]
    n1, n2 = ent[2, 0], ent[2, 1]
    for j, ref in enumerate(c_refs):
        cs[j] = ref[...]
    acc[...] = jnp.zeros(acc.shape, F32)
    starts = quarter_starts(ent[2, 2])
    for ref, start in zip(st_refs, starts):
        st[:, pl.ds(start, QUARTER), :] = ref[...]
    lane = lanes_of(BLK)

    def coefs(k, hit):
        here = lane == group_lane(ent, k, n1)
        m = jnp.max(jnp.where(here, st[0], LOWEST), axis=1, keepdims=True)
        l = jnp.sum(jnp.where(here, st[1], 0.0), axis=1, keepdims=True)
        for ref, start in zip(s_refs, starts):
            tile[pl.ds(start, QUARTER), :] = ref[k]
        g = (0.5 * (jnp.exp(tile[...] - m) * (1.0 / l) - hit)).astype(BF16)
        g_ref[k] = g
        return g

    def first(k, hit):
        acc[ent[0, k]] += dot_nn(coefs(k, hit), cs[ent[1, k]])

    def second(k, hit):
        acc[ent[0, k]] += dot_tn(coefs(k, hit), cs[ent[1, k]])

    def far(fn, k, _):
        fn(k, 0.0)
        return 0

    hit = (prow[...] == lax.broadcasted_iota(jnp.int32, (BLK, BLK), 0)).astype(F32)
    first(0, hit.T)
    lax.fori_loop(1, n1, functools.partial(far, first), 0)
    second(n1, hit)
    lax.fori_loop(n1 + 1, n2, functools.partial(far, second), 0)
    own[...] = INV_TEMP * acc[0]
    for e, out in ((1, p1), (2, p2), (3, p3), (7, m1), (6, m2), (5, m3)):
        out[...] = (INV_TEMP * acc[e]).astype(BF16)
    p4a[...] = (INV_TEMP * acc[4, :HALF]).astype(BF16)
    p4b[...] = (INV_TEMP * acc[4, HALF:]).astype(BF16)


def long_query_grads(cap, ent, scores, stats, pairing, c_parts):
    feats = c_parts[0].shape[-1]
    part = jax.ShapeDtypeStruct((BLK, feats), BF16)
    half = jax.ShapeDtypeStruct((HALF, feats), BF16)
    return pl.pallas_call(
        long_query_grad_kernel,
        out_shape=[
            jax.ShapeDtypeStruct((cap, BLK, BLK), BF16),
            jax.ShapeDtypeStruct((BLK, feats), F32),
            *[part, part, part, half, half, part, part, part],
        ],
        in_specs=[spec_s()] + [spec_v()] * (2 * NX + 1 + NCODE),
        out_specs=[spec_v()] * 10,
        scratch_shapes=[
            VMEM((NY * NC, BLK, feats), BF16),
            VMEM((NZ, BLK, feats), F32),
            VMEM((2, BLK, BLK), F32),
            VMEM((BLK, BLK), F32),
        ],
        compiler_params=grant(10 * 2**20, cap),
        cost_estimate=pl.CostEstimate(flops=10**9, bytes_accessed=12 * 10**6, transcendentals=10**5),
        name="query_grads",
    )(ent, *scores, *stats, pairing, *c_parts)


def near_stats(st, left, right, other):
    two = merge(left, st)
    return jnp.stack(two), jnp.stack(merge(two, right)), jnp.stack(merge(st, other))


def final_stats(three, pair, z1, z2, y1, y2, y3):
    over_z = merge(merge(three, z1), z2)
    over_yc = merge(merge(pair, y1), merge(y2, y3))
    first = lanes_of(QUARTER) < NZ
    return (jnp.stack([jnp.where(first, a, b) for a, b in zip(over_z, over_yc)]),)


def long_exchange(cap, scores, st):
    others = from_others(scores, "x")
    left, right, other = shift(st, "z", 1), shift(st, "z", -1), shift(st, "c", 1)
    like = jax.ShapeDtypeStruct(st.shape, F32)
    two, three, pair = small_kernel(near_stats, "near_stats", [like] * 3, st, left, right, other)
    z1, z2 = shift(three, "z", 3), shift(two, "z", -3)
    y1, y2, y3 = from_others(pair, "y")
    (st,) = small_kernel(final_stats, "final_stats", [like], three, pair, z1, z2, y1, y2, y3)
    return (scores, *others), (st, *from_others(st, "x"))


def long_run(cap, queries, codes, pairing, neg_blocks, neg_count):
    ent, over = build_list(neg_blocks, neg_count)
    with jax.named_scope("gather"):
        q_parts, c_parts, ent = gather(queries, codes, ent)
    o0, o1, o2, o3 = partial_scores(cap, ent, q_parts, c_parts)
    with jax.named_scope("scores_over_x"):
        parts = (o0, shift(o1, "x", 1), shift(o2, "x", 2), shift(o3, "x", -1))
    scores, st = local_stats(cap, ent, parts)
    with jax.named_scope("stats"):
        scores, stats = long_exchange(cap, scores, st)
    g, own_q, p1, p2, p3, p4a, p4b, m1, m2, m3 = long_query_grads(
        cap, ent, scores, stats, pairing, c_parts
    )
    own_c, pc1, pc2, pc3, po = code_grads(ent, g, q_parts)
    with jax.named_scope("reduce"):
        from_z = reduce_queries(g, p1, p2, p3, p4a, p4b, m1, m2, m3)[0]
        from_yc = reduce_codes(po, pc1, pc2, pc3)
    return over, (total(own_q, *from_z), total(own_c, *from_yc))


def local(*args):
    over, short = run(CAP_SMALL, *args)
    return lax.while_loop(
        lambda state: state[0] > 0,
        lambda state: (jnp.int32(0), long_run(CAP_FULL, *args)[1]),
        (over[0], short),
    )[1]


def solution(mesh):
    grid = Mesh(mesh.devices.reshape(NY, NZ, NC, NX), ("y", "z", "c", "x"))
    in_specs = (P(DP, "x"), P(DP, "x"), P(DP, None), P(), P())
    out_specs = (P(DP, "x"), P(DP, "x"))
    return jax.shard_map(local, mesh=grid, in_specs=in_specs, out_specs=out_specs, check_vma=False)
```

```python
import functools

import jax
import jax.numpy as jnp
from jax import lax
from jax.experimental import pallas as pl
from jax.experimental.pallas import tpu as pltpu
from jax.sharding import Mesh, PartitionSpec as P

INV_TEMP = 50.0
NY, NZ, NC, NX = 4, 8, 2, 4
BLK = 128
SLOTS = 4
QUARTER = BLK // NX
HALF = BLK // 2
CAP_SMALL = 18
CAP_FULL = 80
LOWEST = -3.0e38
DP = ("y", "z", "c")
LIST_LEN = 88
GRANT_PER_SLOT = 5 * 2**14
F32 = jnp.float32
BF16 = jnp.bfloat16
VMEM = pltpu.VMEM
SMEM = pltpu.SMEM


def wrap(v, n):
    return v & (n - 1)


def grant(own, cap):
    return pltpu.CompilerParams(vmem_limit_bytes=own + GRANT_PER_SLOT * cap)


def spec_v():
    return pl.BlockSpec(memory_space=VMEM)


def spec_s():
    return pl.BlockSpec(memory_space=SMEM)


def list_kernel(neg_ref, count_ref, neg_v, count_v, ent_ref, over_ref):
    y, z, c, x = (lax.axis_index(name) for name in ("y", "z", "c", "x"))

    def push(k, e, j, take):
        ent_ref[0, k] = e
        ent_ref[1, k] = j
        return k + take.astype(jnp.int32)

    def first(e, k):
        b = ((y << 3) + wrap(z + e, NZ)) * NC + c
        count = count_ref[b]
        for r in range(SLOTS):
            n = neg_ref[r, b]
            take = (r < count) & (wrap(n >> 1, NZ) == z)
            k = push(k, e, 2 * wrap((n >> 4) - y, NY) + ((n & 1) ^ c), take)
        return k

    def second(j, k):
        b = ((wrap(y + (j >> 1), NY) << 3) + z) * NC + ((j & 1) ^ c)
        count = count_ref[b]
        for r in range(SLOTS):
            n = neg_ref[r, b]
            take = (r < count) & ((n >> 4) == y) & ((n & 1) == c)
            k = push(k, wrap((n >> 1) - z, NZ), j, take)
        return k

    n1 = lax.fori_loop(0, NZ, first, push(0, 0, 0, jnp.bool_(True)))
    n2 = lax.fori_loop(0, NY * NC, second, push(n1, 0, 0, jnp.bool_(True)))
    for i, v in enumerate((n1, n2, x, y, z, c)):
        ent_ref[2, i] = v
    blocks = count_v.shape[1]
    shape = (NZ, blocks)
    group = lax.broadcasted_iota(jnp.int32, shape, 0)
    b = lax.broadcasted_iota(jnp.int32, shape, 1)
    count = jnp.broadcast_to(count_v[...], shape)

    def rows_of(n):
        return ((n >> 4) << 1) + (n & 1)

    def cols_of(n):
        return wrap(n >> 1, NZ)

    def ones(mask):
        return jnp.where(mask, 1.0, 0.0)

    to_cols, to_rows = jnp.zeros(shape, F32), jnp.zeros(shape, F32)
    for r in range(SLOTS):
        n = jnp.broadcast_to(neg_v[pl.ds(r, 1), :], shape)
        to_cols += ones((cols_of(n) == group) & (r < count))
        to_rows += ones((rows_of(n) == group) & (r < count))
    tiles = dot_nt(ones(rows_of(b) == group), to_cols) + dot_nt(to_rows, ones(cols_of(b) == group))
    over_ref[0] = (jnp.max(tiles) + 2.0 > CAP_SMALL).astype(jnp.int32)


def build_list(neg_blocks, neg_count):
    neg = neg_blocks.T
    return pl.pallas_call(
        list_kernel,
        out_shape=[
            jax.ShapeDtypeStruct((3, LIST_LEN), jnp.int32),
            jax.ShapeDtypeStruct((1,), jnp.int32),
        ],
        in_specs=[spec_s(), spec_s(), spec_v(), spec_v()],
        out_specs=[spec_s(), spec_s()],
        compiler_params=grant(2 * 2**20, 0),
        name="block_list",
    )(neg, neg_count, neg, neg_count.reshape(1, -1))


NQ, NCODE = 9, 8


def fill_queries(q_refs, qs):
    own, l1, l2, l3, r1, r2, r3, r4, l4 = q_refs
    for e, ref in ((0, own), (1, l1), (2, l2), (3, l3), (7, r1), (6, r2), (5, r3)):
        qs[e] = ref[...]
    qs[4, :HALF] = r4[...]
    qs[4, HALF:] = l4[...]


def dot_nt(a, b):
    return lax.dot_general(a, b, (((1,), (1,)), ((), ())), preferred_element_type=F32)


def dot_nn(a, b):
    return lax.dot_general(a, b, (((1,), (0,)), ((), ())), preferred_element_type=F32)


def dot_tn(a, b):
    return lax.dot_general(a, b, (((0,), (0,)), ((), ())), preferred_element_type=F32)


def quarter_starts(x):
    return [pl.multiple_of(wrap(x + d, NX) * QUARTER, QUARTER) for d in range(NX)]


def score_kernel(ent, *refs):
    q_refs, c_refs = refs[:NQ], refs[NQ : NQ + NCODE]
    outs = refs[NQ + NCODE : NQ + NCODE + NX]
    qs, cs, tile = refs[NQ + NCODE + NX :]
    fill_queries(q_refs, qs)
    for j, ref in enumerate(c_refs):
        cs[j] = ref[...]
    n1, n2 = ent[2, 0], ent[2, 1]
    starts = quarter_starts(ent[2, 2])

    def emit(k, s):
        tile[...] = s
        for out, start in zip(outs, starts):
            out[k] = tile[pl.ds(start, QUARTER), :]

    def first(k, _):
        emit(k, dot_nt(qs[ent[0, k]], cs[ent[1, k]]))
        return 0

    def second(k, _):
        emit(k, dot_nt(cs[ent[1, k]], qs[ent[0, k]]))
        return 0

    lax.fori_loop(0, n1, first, 0)
    lax.fori_loop(n1, n2, second, 0)


def partial_scores(cap, ent, q_parts, c_parts):
    feats = q_parts[0].shape[-1]
    return pl.pallas_call(
        score_kernel,
        out_shape=[jax.ShapeDtypeStruct((cap, QUARTER, BLK), F32)] * NX,
        in_specs=[spec_s()] + [spec_v()] * (NQ + NCODE),
        out_specs=[spec_v()] * NX,
        scratch_shapes=[
            VMEM((NZ, BLK, feats), BF16),
            VMEM((NY * NC, BLK, feats), BF16),
            VMEM((BLK, BLK), F32),
        ],
        compiler_params=grant(8 * 2**20, cap),
        name="scores",
    )(ent, *q_parts, *c_parts)


def group_lane(ent, k, n1):
    y, z, c = ent[2, 3], ent[2, 4], ent[2, 5]
    e, j = ent[0, k], ent[1, k]
    first = wrap(z + e, NZ)
    second = NZ + 2 * wrap(y + (j >> 1), NY) + ((j & 1) ^ c)
    return jnp.where(k < n1, first, second)


def lanes_of(rows):
    return lax.broadcasted_iota(jnp.int32, (rows, BLK), 1)


def stats_kernel(ent, s0, s1, s2, s3, s_ref, st_ref, top, tot):
    n1, n2 = ent[2, 0], ent[2, 1]
    top[...] = jnp.full(top.shape, LOWEST, F32)
    tot[...] = jnp.zeros(tot.shape, F32)

    def first(k, _):
        s = INV_TEMP * ((s0[k] + s2[k]) + (s1[k] + s3[k]))
        s_ref[k] = s
        g = group_lane(ent, k, n1)
        top[g] = jnp.maximum(top[g], s)
        return 0

    lax.fori_loop(0, n2, first, 0)
    for g in range(2 * NZ):
        top[g] = jnp.broadcast_to(jnp.max(top[g], axis=1, keepdims=True), (QUARTER, BLK))

    def second(k, _):
        g = group_lane(ent, k, n1)
        tot[g] = tot[g] + jnp.exp(s_ref[k] - top[g])
        return 0

    lax.fori_loop(0, n2, second, 0)
    lane = lanes_of(QUARTER)
    m = jnp.full((QUARTER, BLK), LOWEST, F32)
    l = jnp.zeros((QUARTER, BLK), F32)
    for g in range(2 * NZ):
        m = jnp.where(lane == g, top[g], m)
        l = jnp.where(lane == g, jnp.sum(tot[g], axis=1, keepdims=True), l)
    st_ref[0] = m
    st_ref[1] = l


def local_stats(cap, ent, parts):
    return pl.pallas_call(
        stats_kernel,
        out_shape=[
            jax.ShapeDtypeStruct((cap, QUARTER, BLK), F32),
            jax.ShapeDtypeStruct((2, QUARTER, BLK), F32),
        ],
        in_specs=[spec_s()] + [spec_v()] * NX,
        out_specs=[spec_v()] * 2,
        scratch_shapes=[VMEM((2 * NZ, QUARTER, BLK), F32)] * 2,
        compiler_params=grant(2 * 2**20, cap),
        name="local_stats",
    )(ent, *parts)


def coef_kernel(ent, s_ref, prow, za, zb, ya, yb, g_ref, top, inv, hits):
    n1, n2 = ent[2, 0], ent[2, 1]
    lane = lanes_of(QUARTER)
    over_z, over_yc = merge(za[...], zb[...]), merge(ya[...], yb[...])
    m, l = (jnp.where(lane < NZ, a, b) for a, b in zip(over_z, over_yc))
    for g in range(2 * NZ):
        here, shape = lane == g, (QUARTER, BLK)
        top[g] = jnp.broadcast_to(jnp.max(jnp.where(here, m, LOWEST), axis=1, keepdims=True), shape)
        inv[g] = jnp.broadcast_to(1.0 / jnp.sum(jnp.where(here, l, 0.0), axis=1, keepdims=True), shape)
    start = pl.multiple_of(ent[2, 2] * QUARTER, QUARTER)
    hit = (prow[...] == lax.broadcasted_iota(jnp.int32, (BLK, BLK), 0)).astype(F32)
    hits[0] = hit.T
    hits[1] = hit

    def probs(k):
        g = group_lane(ent, k, n1)
        return jnp.exp(s_ref[k] - top[g]) * inv[g]

    def far(k, _):
        g_ref[k] = (0.5 * probs(k)).astype(BF16)
        return 0

    lax.fori_loop(1, n1, far, 0)
    lax.fori_loop(n1 + 1, n2, far, 0)
    g_ref[0] = (0.5 * (probs(0) - hits[0, pl.ds(start, QUARTER), :])).astype(BF16)
    g_ref[n1] = (0.5 * (probs(n1) - hits[1, pl.ds(start, QUARTER), :])).astype(BF16)


def coefficients(cap, ent, scores, pairing, *stats):
    return pl.pallas_call(
        coef_kernel,
        out_shape=jax.ShapeDtypeStruct((cap, QUARTER, BLK), BF16),
        in_specs=[spec_s()] + [spec_v()] * 6,
        out_specs=spec_v(),
        scratch_shapes=[
            VMEM((2 * NZ, QUARTER, BLK), F32),
            VMEM((2 * NZ, QUARTER, BLK), F32),
            VMEM((2, BLK, BLK), F32),
        ],
        compiler_params=grant(2 * 2**20, cap),
        name="coefficients",
    )(ent, scores, pairing, *stats)


def query_grad_kernel(ent, *refs):
    quarters, c_refs, refs = refs[:NX], refs[NX : NX + NCODE], refs[NX + NCODE :]
    g_ref, own, p1, p2, p3, p4a, p4b, m1, m2, m3 = refs[:10]
    cs, acc = refs[10:]
    n1, n2 = ent[2, 0], ent[2, 1]
    for j, ref in enumerate(c_refs):
        cs[j] = ref[...]
    acc[...] = jnp.zeros(acc.shape, F32)
    starts = quarter_starts(ent[2, 2])

    def coefs(k):
        for ref, start in zip(quarters, starts):
            g_ref[k, pl.ds(start, QUARTER), :] = ref[k]
        return g_ref[k]

    def first(k, _):
        acc[ent[0, k]] += dot_nn(coefs(k), cs[ent[1, k]])
        return 0

    def second(k, _):
        acc[ent[0, k]] += dot_tn(coefs(k), cs[ent[1, k]])
        return 0

    lax.fori_loop(0, n1, first, 0)
    lax.fori_loop(n1, n2, second, 0)
    own[...] = INV_TEMP * acc[0]
    for e, out in ((1, p1), (2, p2), (3, p3), (7, m1), (6, m2), (5, m3)):
        out[...] = (INV_TEMP * acc[e]).astype(BF16)
    p4a[...] = (INV_TEMP * acc[4, :HALF]).astype(BF16)
    p4b[...] = (INV_TEMP * acc[4, HALF:]).astype(BF16)


def query_grads(cap, ent, coefs, c_parts):
    feats = c_parts[0].shape[-1]
    part = jax.ShapeDtypeStruct((BLK, feats), BF16)
    half = jax.ShapeDtypeStruct((HALF, feats), BF16)
    return pl.pallas_call(
        query_grad_kernel,
        out_shape=[
            jax.ShapeDtypeStruct((cap, BLK, BLK), BF16),
            jax.ShapeDtypeStruct((BLK, feats), F32),
            *[part, part, part, half, half, part, part, part],
        ],
        in_specs=[spec_s()] + [spec_v()] * (NX + NCODE),
        out_specs=[spec_v()] * 10,
        scratch_shapes=[
            VMEM((NY * NC, BLK, feats), BF16),
            VMEM((NZ, BLK, feats), F32),
        ],
        compiler_params=grant(10 * 2**20, cap),
        cost_estimate=pl.CostEstimate(flops=10**9, bytes_accessed=12 * 10**6, transcendentals=0),
        name="query_grads",
    )(ent, *coefs, *c_parts)


def code_grad_kernel(ent, g_ref, *refs):
    q_refs, (own, pc1, pc2, pc3, po, qs, acc) = refs[:NQ], refs[NQ:]
    n1, n2 = ent[2, 0], ent[2, 1]
    fill_queries(q_refs, qs)
    acc[...] = jnp.zeros(acc.shape, F32)

    def first(k, _):
        acc[ent[1, k]] += dot_tn(g_ref[k], qs[ent[0, k]])
        return 0

    def second(k, _):
        acc[ent[1, k]] += dot_nn(g_ref[k], qs[ent[0, k]])
        return 0

    lax.fori_loop(0, n1, first, 0)
    lax.fori_loop(n1, n2, second, 0)
    own[...] = INV_TEMP * acc[0]
    for d, out in ((1, pc1), (2, pc2), (3, pc3)):
        out[...] = (INV_TEMP * acc[2 * d]).astype(BF16)
    for d in range(NY):
        po[d] = (INV_TEMP * acc[2 * d + 1]).astype(BF16)


def code_grads(ent, coefs, q_parts):
    feats = q_parts[0].shape[-1]
    part = jax.ShapeDtypeStruct((BLK, feats), BF16)
    return pl.pallas_call(
        code_grad_kernel,
        out_shape=[
            jax.ShapeDtypeStruct((BLK, feats), F32),
            *[part, part, part],
            jax.ShapeDtypeStruct((NY, BLK, feats), BF16),
        ],
        in_specs=[spec_s()] + [spec_v()] * (1 + NQ),
        out_specs=[spec_v()] * 5,
        scratch_shapes=[VMEM((NZ, BLK, feats), BF16), VMEM((NY * NC, BLK, feats), F32)],
        compiler_params=grant(10 * 2**20, coefs.shape[0]),
        cost_estimate=pl.CostEstimate(flops=10**9, bytes_accessed=12 * 10**6, transcendentals=0),
        name="code_grads",
    )(ent, coefs, *q_parts)


def shift(value, axis, by):
    n = {"x": NX, "y": NY, "z": NZ, "c": NC}[axis]
    return lax.ppermute(value, axis, [(i, (i + by) % n) for i in range(n)])


def merge(a, b):
    m = jnp.maximum(a[0], b[0])
    return m, a[1] * jnp.exp(a[0] - m) + b[1] * jnp.exp(b[0] - m)


def small_kernel(fn, name, out_shape, *args):
    def kernel(*refs):
        outs = fn(*(ref[...] for ref in refs[: len(args)]))
        for ref, out in zip(refs[len(args) :], outs):
            ref[...] = out

    return pl.pallas_call(
        kernel,
        out_shape=out_shape,
        in_specs=[spec_v()] * len(args),
        out_specs=[spec_v()] * len(out_shape),
        compiler_params=grant(4 * 2**20, 0),
        name=name,
    )(*args)


def merge_both(za, zb, ya, yb):
    return jnp.stack(merge(za, zb)), jnp.stack(merge(ya, yb))


def swap(value, axis, bit):
    n = {"y": NY, "z": NZ, "c": NC}[axis]
    return lax.ppermute(value, axis, [(i, i ^ bit) for i in range(n)])


def exchange(st):
    like = [jax.ShapeDtypeStruct(st.shape, F32)] * 2
    over_z, over_yc = st, st
    for z_bit, (axis, bit) in ((1, ("c", 1)), (2, ("y", 1))):
        over_z, over_yc = small_kernel(
            merge_both, "merge", like, over_z, swap(over_z, "z", z_bit), over_yc, swap(over_yc, axis, bit)
        )
    return over_z, swap(over_z, "z", 4), over_yc, swap(over_yc, "y", 2)


def from_others(value, axis):
    return shift(value, axis, -1), shift(value, axis, 2), shift(value, axis, 1)


def gather(queries, codes, ent):
    r1, l1 = shift(queries, "z", 1), shift(queries, "z", -1)
    c_mine = (codes, *from_others(codes, "y"))
    c_parts = tuple(v for part in c_mine for v in (part, shift(part, "c", 1)))
    r1, l1, ent = lax.optimization_barrier((r1, l1, ent))
    r2, l2 = shift(r1, "z", 1), shift(l1, "z", -1)
    r3, l3 = shift(r2, "z", 1), shift(l2, "z", -1)
    r4, l4 = shift(r3[:HALF], "z", 1), shift(l3[HALF:], "z", -1)
    return (queries, l1, l2, l3, r1, r2, r3, r4, l4), c_parts, ent


def total(*parts):
    out = parts[0].astype(F32)
    for p in parts[1:]:
        out = out + p.astype(F32)
    return out


def join_halves(b, d, r, l):
    r = jnp.concatenate([total(b, r[:HALF]).astype(BF16), r[HALF:]], axis=0)
    return r, jnp.concatenate([l[:HALF], total(d, l[HALF:]).astype(BF16)], axis=0)


def join(a, b, r, l):
    return total(a, r).astype(BF16), total(b, l).astype(BF16)


def join_codes(other, *parts):
    return [total(part, other[d + 1]).astype(BF16) for d, part in enumerate(parts)]


def reduce_queries(early, p1, p2, p3, p4a, p4b, m1, m2, m3):
    like = [jax.ShapeDtypeStruct(p1.shape, BF16)] * 2
    r, l = shift(p4a, "z", 1), shift(p4b, "z", -1)
    r, l = small_kernel(join_halves, "join_halves", like, r, l, p3, m3)
    for a, b in ((p2, m2), (p1, m1)):
        r, l = shift(r, "z", 1), shift(l, "z", -1)
        if a is p1:
            r, l, early = lax.optimization_barrier((r, l, early))
        r, l = small_kernel(join, "join", like, r, l, a, b)
    return (shift(r, "z", 1), shift(l, "z", -1)), early


def reduce_codes(po, *parts):
    like = [jax.ShapeDtypeStruct(parts[0].shape, BF16)] * 3
    other = shift(po, "c", 1)
    parts = small_kernel(join_codes, "join_codes", like, other, *parts)
    return other[0], *(shift(part, "y", d + 1) for d, part in enumerate(parts))


def run(cap, queries, codes, pairing, neg_blocks, neg_count):
    ent, over = build_list(neg_blocks, neg_count)
    with jax.named_scope("gather"):
        q_parts, c_parts, ent = gather(queries, codes, ent)
    o0, o1, o2, o3 = partial_scores(cap, ent, q_parts, c_parts)
    with jax.named_scope("scores_over_x"):
        parts = (o0, shift(o1, "x", 1), shift(o2, "x", 2), shift(o3, "x", -1))
    scores, st = local_stats(cap, ent, parts)
    with jax.named_scope("stats"):
        stats = exchange(st)
    coefs = coefficients(cap, ent, scores, pairing, *stats)
    with jax.named_scope("coefs_over_x"):
        coefs = (coefs, *from_others(coefs, "x"))
    g, own_q, *parts = query_grads(cap, ent, coefs, c_parts)
    with jax.named_scope("reduce"):
        own_c, pc1, pc2, pc3, po = code_grads(ent, g, q_parts)
        from_yc = reduce_codes(po, pc1, pc2, pc3)
        from_z, from_yc = reduce_queries(from_yc, *parts)
    return over, (total(own_q, *from_z), total(own_c, *from_yc))


def long_query_grad_kernel(ent, *refs):
    s_refs, st_refs, prow = refs[:NX], refs[NX : 2 * NX], refs[2 * NX]
    c_refs, refs = refs[2 * NX + 1 : 2 * NX + 1 + NCODE], refs[2 * NX + 1 + NCODE :]
    g_ref, own, p1, p2, p3, p4a, p4b, m1, m2, m3 = refs[:10]
    cs, acc, st, tile = refs[10:]
    n1, n2 = ent[2, 0], ent[2, 1]
    for j, ref in enumerate(c_refs):
        cs[j] = ref[...]
    acc[...] = jnp.zeros(acc.shape, F32)
    starts = quarter_starts(ent[2, 2])
    for ref, start in zip(st_refs, starts):
        st[:, pl.ds(start, QUARTER), :] = ref[...]
    lane = lanes_of(BLK)

    def coefs(k, hit):
        here = lane == group_lane(ent, k, n1)
        m = jnp.max(jnp.where(here, st[0], LOWEST), axis=1, keepdims=True)
        l = jnp.sum(jnp.where(here, st[1], 0.0), axis=1, keepdims=True)
        for ref, start in zip(s_refs, starts):
            tile[pl.ds(start, QUARTER), :] = ref[k]
        g = (0.5 * (jnp.exp(tile[...] - m) * (1.0 / l) - hit)).astype(BF16)
        g_ref[k] = g
        return g

    def first(k, hit):
        acc[ent[0, k]] += dot_nn(coefs(k, hit), cs[ent[1, k]])

    def second(k, hit):
        acc[ent[0, k]] += dot_tn(coefs(k, hit), cs[ent[1, k]])

    def far(fn, k, _):
        fn(k, 0.0)
        return 0

    hit = (prow[...] == lax.broadcasted_iota(jnp.int32, (BLK, BLK), 0)).astype(F32)
    first(0, hit.T)
    lax.fori_loop(1, n1, functools.partial(far, first), 0)
    second(n1, hit)
    lax.fori_loop(n1 + 1, n2, functools.partial(far, second), 0)
    own[...] = INV_TEMP * acc[0]
    for e, out in ((1, p1), (2, p2), (3, p3), (7, m1), (6, m2), (5, m3)):
        out[...] = (INV_TEMP * acc[e]).astype(BF16)
    p4a[...] = (INV_TEMP * acc[4, :HALF]).astype(BF16)
    p4b[...] = (INV_TEMP * acc[4, HALF:]).astype(BF16)


def long_query_grads(cap, ent, scores, stats, pairing, c_parts):
    feats = c_parts[0].shape[-1]
    part = jax.ShapeDtypeStruct((BLK, feats), BF16)
    half = jax.ShapeDtypeStruct((HALF, feats), BF16)
    return pl.pallas_call(
        long_query_grad_kernel,
        out_shape=[
            jax.ShapeDtypeStruct((cap, BLK, BLK), BF16),
            jax.ShapeDtypeStruct((BLK, feats), F32),
            *[part, part, part, half, half, part, part, part],
        ],
        in_specs=[spec_s()] + [spec_v()] * (2 * NX + 1 + NCODE),
        out_specs=[spec_v()] * 10,
        scratch_shapes=[
            VMEM((NY * NC, BLK, feats), BF16),
            VMEM((NZ, BLK, feats), F32),
            VMEM((2, BLK, BLK), F32),
            VMEM((BLK, BLK), F32),
        ],
        compiler_params=grant(10 * 2**20, cap),
        cost_estimate=pl.CostEstimate(flops=10**9, bytes_accessed=12 * 10**6, transcendentals=10**5),
        name="query_grads",
    )(ent, *scores, *stats, pairing, *c_parts)


def near_stats(st, left, right, other):
    two = merge(left, st)
    return jnp.stack(two), jnp.stack(merge(two, right)), jnp.stack(merge(st, other))


def final_stats(three, pair, z1, z2, y1, y2, y3):
    over_z = merge(merge(three, z1), z2)
    over_yc = merge(merge(pair, y1), merge(y2, y3))
    first = lanes_of(QUARTER) < NZ
    return (jnp.stack([jnp.where(first, a, b) for a, b in zip(over_z, over_yc)]),)


def long_exchange(cap, scores, st):
    others = from_others(scores, "x")
    left, right, other = shift(st, "z", 1), shift(st, "z", -1), shift(st, "c", 1)
    like = jax.ShapeDtypeStruct(st.shape, F32)
    two, three, pair = small_kernel(near_stats, "near_stats", [like] * 3, st, left, right, other)
    z1, z2 = shift(three, "z", 3), shift(two, "z", -3)
    y1, y2, y3 = from_others(pair, "y")
    (st,) = small_kernel(final_stats, "final_stats", [like], three, pair, z1, z2, y1, y2, y3)
    return (scores, *others), (st, *from_others(st, "x"))


def long_run(cap, queries, codes, pairing, neg_blocks, neg_count):
    ent, over = build_list(neg_blocks, neg_count)
    with jax.named_scope("gather"):
        q_parts, c_parts, ent = gather(queries, codes, ent)
    o0, o1, o2, o3 = partial_scores(cap, ent, q_parts, c_parts)
    with jax.named_scope("scores_over_x"):
        parts = (o0, shift(o1, "x", 1), shift(o2, "x", 2), shift(o3, "x", -1))
    scores, st = local_stats(cap, ent, parts)
    with jax.named_scope("stats"):
        scores, stats = long_exchange(cap, scores, st)
    g, own_q, p1, p2, p3, p4a, p4b, m1, m2, m3 = long_query_grads(
        cap, ent, scores, stats, pairing, c_parts
    )
    own_c, pc1, pc2, pc3, po = code_grads(ent, g, q_parts)
    with jax.named_scope("reduce"):
        from_z = reduce_queries(g, p1, p2, p3, p4a, p4b, m1, m2, m3)[0]
        from_yc = reduce_codes(po, pc1, pc2, pc3)
    return over, (total(own_q, *from_z), total(own_c, *from_yc))


def local(*args):
    over, short = run(CAP_SMALL, *args)
    return lax.while_loop(
        lambda state: state[0] > 0,
        lambda state: (jnp.int32(0), long_run(CAP_FULL, *args)[1]),
        (over[0], short),
    )[1]


def solution(mesh):
    grid = Mesh(mesh.devices.reshape(NY, NZ, NC, NX), ("y", "z", "c", "x"))
    in_specs = (P(DP, "x"), P(DP, "x"), P(DP, None), P(), P())
    out_specs = (P(DP, "x"), P(DP, "x"))
    return jax.shard_map(local, mesh=grid, in_specs=in_specs, out_specs=out_specs, check_vma=False)
```
